512 devices in a mesh: gx: 64 (over z, x_hi, core), gy: 8 (over y, x_lo).
Axes of the slice: x: 4 (x_hi: 2, x_lo: 2; x = x_hi * 2 + x_lo), y: 4, z: 16, core: 2. Of those that a mesh axis runs over, the one named last changes fastest.
Arguments:
- tokens: bfloat16 [512, 8192], P('gx', 'gy'), may hold values from -6 to 6
- out_grad: bfloat16 [512, 8192], P('gx', 'gy'), may hold values from -6 to 6
- gate_weight: bfloat16 [8192, 16384], P('gy', 'gx'), may hold values from -0.0625 to 0.0625
- up_weight: bfloat16 [8192, 16384], P('gy', 'gx'), may hold values from -0.0625 to 0.0625
- down_weight: bfloat16 [16384, 8192], P('gx', 'gy'), may hold values from -0.046875 to 0.046875
Outputs:
- input_grad: bfloat16 [512, 8192], P('gx', 'gy')
- gate_grad: bfloat16 [8192, 16384], P('gy', 'gx')
- up_grad: bfloat16 [8192, 16384], P('gy', 'gx')
- down_grad: bfloat16 [16384, 8192], P('gx', 'gy')
The draws below stay inside these ranges and needn't reach their ends.
All inputs are finite; a program needn't handle non-finite values.
Results may differ from the reference program's by a relative error of at most 0.0049.
Values may be sent and summed in bfloat16 or wider, within the bound.
A program may use at most 64 MiB of HBM per device.

```python
import jax
import jax.numpy as jnp
from jax import lax

D = 8192
FF = 16384
ROWS = 512


def block_levels(rng, shape, shards, least, high):
    def one(axis_at, shards_of):
        steps = jax.random.uniform(jax.random.fold_in(jax.random.fold_in(rng, 6), axis_at), (shards_of,), jnp.float32, least / len(shards), high / len(shards))
        return jnp.repeat(jnp.exp(steps), shape[axis_at] // shards_of).reshape((-1,) + (1,) * (len(shape) - axis_at - 1))

    loudness = one(*shards[0])
    for cut in shards[1:]:
        loudness = loudness * one(*cut)
    return loudness


def centred(rng, extent, deviation, most, pieces=(), held_as=jnp.bfloat16):
    entries = deviation * jax.random.normal(rng, extent, jnp.float32)
    if pieces:
        entries = entries * block_levels(rng, extent, pieces, -0.22, 0.18)
    return jnp.clip(entries, -most, most).astype(held_as)


def setup_inputs(seed: int = 0) -> dict:
    seeds = jax.random.split(jax.random.key(seed), 6)
    tokens = centred(seeds[0], (ROWS, D), 1.0, 6.0, ((0, 64), (1, 8)))
    out_grad = centred(seeds[1], (ROWS, D), 1.0, 6.0, ((0, 64), (1, 8)))
    gate_weight = centred(seeds[2], (D, FF), D ** -0.5, 0.0625, ((0, 8), (1, 64)))
    up_weight = centred(seeds[3], (D, FF), D ** -0.5, 0.0625, ((0, 8), (1, 64)))
    down_weight = centred(seeds[4], (FF, D), FF ** -0.5, 0.046875, ((0, 64), (1, 8)))
    return dict(tokens=tokens, out_grad=out_grad, gate_weight=gate_weight, up_weight=up_weight, down_weight=down_weight)


def reference(tokens, out_grad, gate_weight, up_weight, down_weight):
    gate = jnp.dot(tokens, gate_weight, preferred_element_type=jnp.float32)
    up = jnp.dot(tokens, up_weight, preferred_element_type=jnp.float32)
    hidden_grad = lax.dot_general(out_grad, down_weight, (((1,), (1,)), ((), ())), preferred_element_type=jnp.float32)
    sigma = jax.nn.sigmoid(gate)
    active = gate * sigma
    hidden = (active * up).astype(jnp.bfloat16)
    dgate = (hidden_grad * up * sigma * (1.0 + gate * (1.0 - sigma))).astype(jnp.bfloat16)
    dup = (hidden_grad * active).astype(jnp.bfloat16)
    factor = 1.0 / jnp.sqrt(jnp.float32(tokens.shape[0]))
    down_grad = (lax.dot_general(hidden, out_grad, (((0,), (0,)), ((), ())), preferred_element_type=jnp.float32) * factor).astype(jnp.bfloat16)
    gate_grad = (lax.dot_general(tokens, dgate, (((0,), (0,)), ((), ())), preferred_element_type=jnp.float32) * factor).astype(jnp.bfloat16)
    up_grad = (lax.dot_general(tokens, dup, (((0,), (0,)), ((), ())), preferred_element_type=jnp.float32) * factor).astype(jnp.bfloat16)
    input_grad = lax.dot_general(dgate, gate_weight, (((1,), (1,)), ((), ())), preferred_element_type=jnp.float32)
    input_grad = input_grad + lax.dot_general(dup, up_weight, (((1,), (1,)), ((), ())), preferred_element_type=jnp.float32)
    return (input_grad.astype(jnp.bfloat16), gate_grad, up_grad, down_grad)
```

```python
import jax
import jax.numpy as jnp
from jax import lax
from jax.experimental import pallas as pl
from jax.experimental.pallas import tpu as pltpu
from jax.sharding import PartitionSpec as P

MESH = pl.DeviceIdType.MESH
BF16, F32 = jnp.bfloat16, jnp.float32

NEAR = (0, 1, -1, 2)
FAR_ORDER = (2, 1, 3)
NEAR_ORDER = (3, 1, 2)


def dot(a, b, dims):
    return lax.dot_general(a, b, (dims, ((), ())), preferred_element_type=F32)


def kernel(tok_ref, grad_ref, gw_hbm, uw_hbm, dw_hbm,
           ig_ref, gg_ref, ug_ref, dg_ref,
           gw, uw, dw, ex_out, ex_in, x, part, b_in, h, ig, core_in,
           near_out, near_own, near_in, far_out, far_in,
           w_sem, send_sem, recv_sem):
    gx, gy = lax.axis_index("gx"), lax.axis_index("gy")
    z, xh, c = gx // 4, (gx // 2) % 2, gx % 2
    y, xl = gy // 2, gy % 2

    def along(dz=0, other_x=False, other_core=False):
        zz = (z + dz + 16) % 16
        xx = 1 - xh if other_x else xh
        cc = 1 - c if other_core else c
        return (zz * 4 + xx * 2 + cc, gy)

    peers = [(dy, dx) for dy in (2, 1, 3, 0) for dx in (1, 0) if dy or dx]

    def across(dy, dx):
        return ((y + dy) % 4) * 2 + (xl + dx) % 2

    loads = [pltpu.make_async_copy(s, d, w_sem.at[i])
             for i, (s, d) in enumerate(((gw_hbm, gw), (uw_hbm, uw), (dw_hbm, dw)))]
    for cp in loads:
        cp.start()

    barrier = pltpu.get_barrier_semaphore()
    met = [along(dz) for dz in (8, 4, -4, 2, -2, 1, -1)]
    met += [along(dz, other_x=True) for dz in (8, 4, -4, 0)]
    met += [along(other_core=True)]
    met += [(gx, across(dy, dx)) for dy, dx in peers]
    for dev in met:
        pl.semaphore_signal(barrier, inc=1, device_id=dev, device_id_type=MESH)

    first = c == 0
    tok, grad = tok_ref[...].astype(F32), grad_ref[...].astype(F32)
    mine = jnp.where(first, tok, grad)
    ex_out[...] = jnp.where(first, grad, tok)
    pl.semaphore_wait(barrier, len(met))

    sent = []

    def push(src, dst, dev):
        k = len(sent)
        cp = pltpu.make_async_remote_copy(
            src_ref=src, dst_ref=dst, send_sem=send_sem.at[k], recv_sem=recv_sem.at[k],
            device_id=dev, device_id_type=MESH)
        cp.start()
        sent.append(cp)
        return cp

    sibling = along(other_core=True)
    partner = along(other_x=True)

    push(ex_out, ex_in, sibling).wait_recv()
    theirs = ex_in[...]
    block = jnp.concatenate(
        [jnp.where(first, mine, theirs), jnp.where(first, theirs, mine)], axis=0)
    x[c, 0, 0, 0] = block.astype(BF16)

    far = [push(x.at[c, 0, 0, 0], x.at[c, 0, 0, 4 - i], along(4 * i)) for i in FAR_ORDER]
    for cp in far:
        cp.wait_recv()
    near = [push(x.at[c, 0, 0], x.at[c, 0, n], along(-NEAR[n])) for n in NEAR_ORDER]
    to_x = [push(x.at[c, 0, 0], x.at[c, 1, 0], partner)]
    to_core = [push(x.at[c, 0, 0], x.at[c, 0, 0], sibling)]
    for n, cp in zip((1, 2, 3), (near[1], near[2], near[0])):
        cp.wait_recv()
        to_x.append(push(x.at[c, 0, n], x.at[c, 1, n], partner))
        to_core.append(push(x.at[c, 0, n], x.at[c, 0, n], sibling))

    def products(k):
        rows = x[0, k].reshape(256, 1024)
        part[k, :, :, 0:256] = dot(rows, gw[...], ((1,), (0,))).reshape(8, 32, 256)
        part[k, :, :, 256:512] = dot(rows, uw[...], ((1,), (0,))).reshape(8, 32, 256)
        part[k, :, :, 512:768] = dot(
            x[1, k].reshape(256, 1024), dw[...], ((1,), (1,))).reshape(8, 32, 256)
        return [push(part.at[k, across(dy, dx)], b_in.at[k, s], (gx, across(dy, dx)))
                for s, (dy, dx) in enumerate(peers)]

    def pointwise(k, arrived):
        for cp in arrived:
            cp.wait_recv()
        total = part[k, gy]
        for s in range(7):
            total = total + b_in[k, s]
        gate, up, hgrad = total[:, 0:256], total[:, 256:512], total[:, 512:768]
        sigma = jax.nn.sigmoid(gate)
        act = gate * sigma
        h[k, gy, :, 0:256] = (act * up).astype(BF16)
        h[k, gy, :, 256:512] = (hgrad * up * sigma * (1.0 + gate * (1.0 - sigma))).astype(BF16)
        h[k, gy, :, 512:768] = (hgrad * act).astype(BF16)
        return [push(h.at[k, gy], h.at[k, gy], (gx, across(dy, dx))) for dy, dx in peers]

    def input_products(k, arrived):
        for cp in arrived:
            cp.wait_recv()
        hh = h[k].reshape(256, 768)
        for j in range(2):
            cols = slice(512 * j, 512 * j + 512)
            v = dot(hh[:, 256:512], gw[cols, :], ((1,), (1,)))
            v = v + dot(hh[:, 512:768], uw[cols, :], ((1,), (1,)))
            ig[k, :, :, :, cols] = v.reshape(16, 2, 8, 512)
        return push(ig.at[k, :, 1 - c], core_in.at[k], sibling)

    def send_near(k, arrived):
        arrived.wait_recv()
        for n in range(4):
            for f in range(4):
                s = 4 * n + f
                v = ig[k, s, c] + core_in[k, s]
                v = jnp.concatenate([v[:, 0:512], v[:, 512:1024]], axis=0)
                if n == 0:
                    near_own[k, f] = v
                else:
                    near_out[k, n, f] = v.astype(BF16)
        return [push(near_out.at[k, n], near_in.at[k, n], along(NEAR[n])) for n in NEAR_ORDER]

    def send_far(k, arrived):
        for cp in arrived:
            cp.wait_recv()
        for f in range(4):
            v = near_own[k, f]
            for n in (1, 2, 3):
                v = v + near_in[k, n, f].astype(F32)
            if k == 0 and f == 0:
                near_own[k, f] = v
            else:
                far_out[k, f] = v.astype(BF16)
        order = FAR_ORDER if k == 0 else FAR_ORDER + (0,)
        return [push(far_out.at[k, f], far_in.at[k, f], along(4 * f, other_x=k == 1))
                for f in order]

    for cp in loads:
        cp.wait()
    for cp in to_core:
        cp.wait_recv()
    b0 = products(0)

    to_core = []
    for n in range(4):
        to_x[n].wait_recv()
        to_core.append(push(x.at[c, 1, n], x.at[c, 1, n], sibling))
    for cp in to_core:
        cp.wait_recv()
    b1 = products(1)

    c0 = pointwise(0, b0)
    c1 = pointwise(1, b1)
    i0 = input_products(0, c0)
    n0 = send_near(0, i0)
    i1 = input_products(1, c1)
    n1 = send_near(1, i1)
    f0 = send_far(0, n0)
    f1 = send_far(1, n1)

    factor = 1.0 / jnp.sqrt(F32(512))

    @pl.loop(0, 4)
    def _(i):
        cols = pl.ds(pl.multiple_of(i * 256, 256), 256)
        hh = h[...].reshape(512, 768)
        t = x[0, :, :, :, :, cols].reshape(512, 256)
        gg_ref[cols, :] = (dot(t, hh[:, 256:512], ((0,), (0,))) * factor).astype(BF16)
        ug_ref[cols, :] = (dot(t, hh[:, 512:768], ((0,), (0,))) * factor).astype(BF16)
        g = x[1, :, :, :, :, cols].reshape(512, 256)
        dg_ref[:, cols] = (dot(hh[:, 0:256], g, ((0,), (0,))) * factor).astype(BF16)

    for cp in f0 + f1:
        cp.wait_recv()
    v = near_own[0, 0] + far_in[1, 0].astype(F32)
    for f in (1, 2, 3):
        v = v + (far_in[0, f].astype(F32) + far_in[1, f].astype(F32))
    ig_ref[...] = jnp.concatenate([v[0:8], v[8:16]], axis=1).astype(BF16)

    for cp in sent:
        cp.wait_send()


COPIES = 62


def per_device(tokens, out_grad, gate_weight, up_weight, down_weight):
    vmem = pl.BlockSpec(memory_space=pltpu.VMEM)
    hbm = pl.BlockSpec(memory_space=pl.ANY)
    shape = jax.ShapeDtypeStruct
    return pl.pallas_call(
        kernel,
        out_shape=(shape((8, 1024), BF16), shape((1024, 256), BF16),
                   shape((1024, 256), BF16), shape((256, 1024), BF16)),
        in_specs=[vmem, vmem, hbm, hbm, hbm],
        out_specs=(vmem,) * 4,
        scratch_shapes=[
            pltpu.VMEM((1024, 256), BF16),
            pltpu.VMEM((1024, 256), BF16),
            pltpu.VMEM((256, 1024), BF16),
            pltpu.VMEM((8, 1024), F32),
            pltpu.VMEM((8, 1024), F32),
            pltpu.VMEM((2, 2, 4, 4, 16, 1024), BF16),
            pltpu.VMEM((2, 8, 32, 768), F32),
            pltpu.VMEM((2, 7, 32, 768), F32),
            pltpu.VMEM((2, 8, 32, 768), BF16),
            pltpu.VMEM((2, 16, 2, 8, 1024), F32),
            pltpu.VMEM((2, 16, 8, 1024), F32),
            pltpu.VMEM((2, 4, 4, 16, 512), BF16),
            pltpu.VMEM((2, 4, 16, 512), F32),
            pltpu.VMEM((2, 4, 4, 16, 512), BF16),
            pltpu.VMEM((2, 4, 16, 512), BF16),
            pltpu.VMEM((2, 4, 16, 512), BF16),
            pltpu.SemaphoreType.DMA((3,)),
            pltpu.SemaphoreType.DMA((COPIES,)),
            pltpu.SemaphoreType.DMA((COPIES,)),
        ],
        compiler_params=pltpu.CompilerParams(
            collective_id=0, has_side_effects=True, vmem_limit_bytes=48 << 20),
        cost_estimate=pl.CostEstimate(
            flops=2 * 8 * 512 * 1024 * 256, bytes_accessed=4 << 20, transcendentals=64 * 256),
    )(tokens, out_grad, gate_weight, up_weight, down_weight)


def solution(mesh):
    return jax.shard_map(
        per_device,
        mesh=mesh,
        in_specs=(P("gx", "gy"), P("gx", "gy"), P("gy", "gx"), P("gy", "gx"), P("gx", "gy")),
        out_specs=(P("gx", "gy"), P("gy", "gx"), P("gy", "gx"), P("gx", "gy")),
        check_vma=False,
    )
```

```python
import jax
import jax.numpy as jnp
from jax import lax
from jax.experimental import pallas as pl
from jax.experimental.pallas import tpu as pltpu
from jax.sharding import PartitionSpec as P

MESH = pl.DeviceIdType.MESH
BF16, F32 = jnp.bfloat16, jnp.float32

NEAR = (0, 1, -1, 2)
FAR_ORDER = (2, 1, 3)
CHUNKS = range(4)
COPIES = 96


def dot(a, b, dims):
    return lax.dot_general(a, b, (dims, ((), ())), preferred_element_type=F32)


def kernel(tok_hbm, grad_hbm, gw_hbm, uw_hbm, dw_hbm,
           ig_hbm, gg_hbm, ug_hbm, dg_hbm,
           tok_v, grad_v, gw, uw, dw, ex_out, ex_in, x, part, b_relay, b_sum, b_in, h,
           ig, core_in, near_out, near_own, near_in, far_out, far_in,
           ig_v, gg_v, ug_v, dg_v,
           load_sem, store_sem, send_sem, recv_sem):
    gx, gy = lax.axis_index("gx"), lax.axis_index("gy")
    z, xh, c = gx // 4, (gx // 2) % 2, gx % 2
    y, xl = gy // 2, gy % 2
    up_y, down_y = (y + 1) % 4, (y + 3) % 4

    def along(dz=0, other_x=False, other_core=False):
        zz = (z + dz + 16) % 16
        xx = 1 - xh if other_x else xh
        cc = 1 - c if other_core else c
        return (zz * 4 + xx * 2 + cc, gy)

    def at(yy, xx):
        return (gx, yy * 2 + xx)

    loads = [pltpu.make_async_copy(s, d, load_sem.at[i]) for i, (s, d) in enumerate((
        (tok_hbm, tok_v), (grad_hbm, grad_v), (gw_hbm, gw), (uw_hbm, uw), (dw_hbm, dw)))]
    for cp in loads:
        cp.start()

    barrier = pltpu.get_barrier_semaphore()
    met = [along(dz) for dz in (8, 4, -4, 2, -2, 1, -1)]
    met += [along(dz, other_x=True) for dz in (8, 4, -4, 0)]
    met += [at(yy, xx) for yy in (up_y, down_y) for xx in (0, 1)] + [at(y, 1 - xl)]
    met += [along(other_core=True)]
    for dev in met:
        pl.semaphore_signal(barrier, inc=1, device_id=dev, device_id_type=MESH)

    loads[0].wait()
    loads[1].wait()
    first = c == 0
    tok, grad = tok_v[...].astype(F32), grad_v[...].astype(F32)
    mine = jnp.where(first, tok, grad)
    ex_out[...] = jnp.where(first, grad, tok)
    pl.semaphore_wait(barrier, len(met))

    sent = []
    marks = [0]

    def reserve(count):
        marks[0] += count
        return marks[0] - count

    def push(src, dst, dev, r=None):
        r = reserve(1) if r is None else r
        cp = pltpu.make_async_remote_copy(
            src_ref=src, dst_ref=dst, send_sem=send_sem.at[len(sent)],
            recv_sem=recv_sem.at[r], device_id=dev, device_id_type=MESH)
        cp.start()
        sent.append(cp)
        return cp

    def arrival(dst, r):
        pltpu.make_async_remote_copy(
            src_ref=dst, dst_ref=dst, send_sem=send_sem.at[0], recv_sem=recv_sem.at[r],
            device_id=at(y, 1 - xl), device_id_type=MESH).wait_recv()

    sibling = along(other_core=True)
    partner = along(other_x=True)

    push(ex_out, ex_in, sibling).wait_recv()
    theirs = ex_in[...]
    block = jnp.concatenate(
        [jnp.where(first, mine, theirs), jnp.where(first, theirs, mine)], axis=0)
    x[c, 0, 0, 0] = block.astype(BF16)

    far = [push(x.at[c, 0, 0, 0], x.at[c, 0, 0, 4 - i], along(4 * i)) for i in FAR_ORDER]
    for cp in far:
        cp.wait_recv()

    def share(n, fs):
        ours = x.at[c, n, 0, fs]
        return push(ours, ours, sibling), push(ours, x.at[c, n, 1, fs], partner)

    whole, low, high = pl.ds(0, 4), pl.ds(0, 2), pl.ds(2, 2)
    near = {3: [push(x.at[c, 0, 0, pl.ds(1, 2)], x.at[c, 3, 0, low], along(2)),
                push(x.at[c, 0, 0, high], x.at[c, 3, 0, high], along(-2))]}
    for n in (1, 2):
        near[n] = [push(x.at[c, 0, 0], x.at[c, n, 0], along(-NEAR[n]))]
    shared = {0: [(whole, share(0, whole))]}
    for n in (1, 2, 3):
        shared[n] = []
        for fs, cp in zip((whole,) if n < 3 else (low, high), near[n]):
            cp.wait_recv()
            shared[n].append((fs, share(n, fs)))

    def rows_ready(n):
        passed = []
        for fs, (from_core, from_x) in shared[n]:
            from_x.wait_recv()
            other = x.at[c, n, 1, fs]
            passed += [from_core, push(other, other, sibling)]
        for cp in passed:
            cp.wait_recv()

    b_base = [reserve(7) for _ in CHUNKS]
    c_base = [reserve(7) for _ in CHUNKS]

    def products(n):
        rows = x[0, n].reshape(128, 1024)
        part[n, :, :, 0:256] = dot(rows, gw[...], ((1,), (0,))).reshape(8, 16, 256)
        part[n, :, :, 256:512] = dot(rows, uw[...], ((1,), (0,))).reshape(8, 16, 256)
        part[n, :, :, 512:768] = dot(
            x[1, n].reshape(128, 1024), dw[...], ((1,), (1,))).reshape(8, 16, 256)
        b = b_base[n]
        across = ((y + 2) % 4) * 2
        push(part.at[n, across], b_relay.at[n, 0], at(up_y, xl), b)
        push(part.at[n, across + 1], b_relay.at[n, 1], at(down_y, xl), b + 1)
        push(part.at[n, up_y * 2 + 1], b_in.at[n, xl], at(up_y, 1), b + 2 + xl)
        push(part.at[n, down_y * 2], b_in.at[n, 2 + xl], at(down_y, 0), b + 4 + xl)
        push(part.at[n, y * 2 + 1 - xl], b_in.at[n, 4], at(y, 1 - xl), b + 6)

    def relay_sums(n):
        b = b_base[n]
        arrival(b_relay.at[n, 0], b)
        b_sum[n, 0] = b_relay[n, 0] + part[n, up_y * 2]
        push(b_sum.at[n, 0], b_in.at[n, xl], at(up_y, 0), b + 2 + xl)
        arrival(b_relay.at[n, 1], b + 1)
        b_sum[n, 1] = b_relay[n, 1] + part[n, down_y * 2 + 1]
        push(b_sum.at[n, 1], b_in.at[n, 2 + xl], at(down_y, 1), b + 4 + xl)

    def pointwise(n):
        total = part[n, gy]
        for s in range(5):
            arrival(b_in.at[n, s], b_base[n] + 2 + s)
        for s in range(5):
            total = total + b_in[n, s]
        gate, up, hgrad = total[:, 0:256], total[:, 256:512], total[:, 512:768]
        sigma = jax.nn.sigmoid(gate)
        act = gate * sigma
        h[n, gy, :, 0:256] = (act * up).astype(BF16)
        h[n, gy, :, 256:512] = (hgrad * up * sigma * (1.0 + gate * (1.0 - sigma))).astype(BF16)
        h[n, gy, :, 512:768] = (hgrad * act).astype(BF16)
        r, ours = c_base[n], h.at[n, gy]
        push(ours, ours, at(up_y, xl), r + xl)
        push(ours, ours, at(down_y, xl), r + 2 + xl)
        push(ours, ours, at(up_y, 1 - xl), r + xl)
        push(ours, ours, at(down_y, 1 - xl), r + 2 + xl)
        push(ours, ours, at(y, 1 - xl), r + 4)

    def relay_hidden(n):
        r = c_base[n]
        piece = h.at[n, down_y * 2]
        arrival(piece, r)
        push(piece, piece, at(up_y, xl), r + 5)
        piece = h.at[n, up_y * 2 + 1]
        arrival(piece, r + 3)
        push(piece, piece, at(down_y, xl), r + 6)

    def input_products(n):
        r = c_base[n]
        arrival(h.at[n, down_y * 2 + 1], r + 1)
        arrival(h.at[n, up_y * 2], r + 2)
        arrival(h.at[n, y * 2 + 1 - xl], r + 4)
        across = ((y + 2) % 4) * 2
        arrival(h.at[n, across], r + 5)
        arrival(h.at[n, across + 1], r + 6)
        hh = h[n].reshape(128, 768)
        for j in range(2):
            cols = slice(512 * j, 512 * j + 512)
            v = dot(hh[:, 256:512], gw[cols, :], ((1,), (1,)))
            v = v + dot(hh[:, 512:768], uw[cols, :], ((1,), (1,)))
            ig[n, :, :, :, cols] = v.reshape(8, 2, 8, 512)
        return push(ig.at[n, :, 1 - c], core_in.at[n], sibling)

    def send_near(n, cp):
        cp.wait_recv()
        for o in range(2):
            for f in range(4):
                v = ig[n, 4 * o + f, c] + core_in[n, 4 * o + f]
                v = jnp.concatenate([v[:, 0:512], v[:, 512:1024]], axis=0)
                if n == 0:
                    near_own[f, o] = v
                else:
                    near_out[n - 1, f, o] = v.astype(BF16)
        if n == 0:
            return []
        if n < 3:
            return [push(near_out.at[n - 1], near_in.at[n - 1], along(NEAR[n]))]
        return [push(near_out.at[2, low], near_in.at[2, low], along(2)),
                push(near_out.at[2, high], near_in.at[2, high], along(-2))]

    for cp in loads[2:]:
        cp.wait()
    core_sent = {}
    near_sent = []
    rows_ready(0)
    products(0)
    rows_ready(1)
    relay_sums(0)
    products(1)
    rows_ready(2)
    pointwise(0)
    products(2)
    relay_sums(1)
    rows_ready(3)
    relay_hidden(0)
    products(3)
    pointwise(1)
    relay_sums(2)
    core_sent[0] = input_products(0)
    relay_hidden(1)
    relay_sums(3)
    pointwise(2)
    near_sent += send_near(0, core_sent[0])
    core_sent[1] = input_products(1)
    pointwise(3)
    relay_hidden(2)
    near_sent += send_near(1, core_sent[1])
    core_sent[2] = input_products(2)
    relay_hidden(3)
    near_sent += send_near(2, core_sent[2])
    core_sent[3] = input_products(3)
    near_sent += send_near(3, core_sent[3])
    for cp in near_sent:
        cp.wait_recv()

    far_sent = []
    for f in FAR_ORDER + (0,):
        for o in range(2):
            v = near_own[f, o]
            for n in (0, 1):
                v = v + near_in[n, f, o].astype(F32)
            if f < 2:
                v = v + near_in[2, f, o].astype(F32)
            if f in (0, 3):
                v = v + near_in[2, (f + 3) % 4, o].astype(F32)
            if o == 0 and f == 0:
                near_own[f, o] = v
            else:
                far_out[f, o] = v.astype(BF16)
                far_sent.append(push(
                    far_out.at[f, o], far_in.at[f, o], along(4 * f, other_x=o == 1)))

    factor = 1.0 / jnp.sqrt(F32(512))

    @pl.loop(0, 4)
    def _(i):
        cols = pl.ds(pl.multiple_of(i * 256, 256), 256)
        hh = h[...].reshape(512, 768)
        t = x[0, :, :, :, :, cols].reshape(512, 256)
        gg_v[cols, :] = (dot(t, hh[:, 256:512], ((0,), (0,))) * factor).astype(BF16)
        ug_v[cols, :] = (dot(t, hh[:, 512:768], ((0,), (0,))) * factor).astype(BF16)
        g = x[1, :, :, :, :, cols].reshape(512, 256)
        dg_v[:, cols] = (dot(hh[:, 0:256], g, ((0,), (0,))) * factor).astype(BF16)

    stores = [pltpu.make_async_copy(s, d, store_sem.at[i]) for i, (s, d) in enumerate((
        (gg_v, gg_hbm), (ug_v, ug_hbm), (dg_v, dg_hbm), (ig_v, ig_hbm)))]
    for cp in stores[:3]:
        cp.start()
    for cp in far_sent:
        cp.wait_recv()
    v = near_own[0, 0] + far_in[0, 1].astype(F32)
    for f in (1, 2, 3):
        v = v + (far_in[f, 0].astype(F32) + far_in[f, 1].astype(F32))
    ig_v[...] = jnp.concatenate([v[0:8], v[8:16]], axis=1).astype(BF16)
    stores[3].start()
    for cp in sent:
        cp.wait_send()
    for cp in stores:
        cp.wait()


def place(a, b, c, d, ao, bo, co, do, sem):
    copies = [pltpu.make_async_copy(s, t, sem.at[i])
              for i, (s, t) in enumerate(((b, bo), (c, co), (d, do), (a, ao)))]
    for cp in copies:
        cp.start()
    for cp in copies:
        cp.wait()


def per_device(tokens, out_grad, gate_weight, up_weight, down_weight):
    hbm = pl.BlockSpec(memory_space=pl.ANY)
    shape = jax.ShapeDtypeStruct
    outs = (shape((8, 1024), BF16), shape((1024, 256), BF16),
            shape((1024, 256), BF16), shape((256, 1024), BF16))
    results = pl.pallas_call(
        kernel,
        out_shape=outs,
        in_specs=[hbm] * 5,
        out_specs=(hbm,) * 4,
        scratch_shapes=[
            pltpu.VMEM((8, 1024), BF16),
            pltpu.VMEM((8, 1024), BF16),
            pltpu.VMEM((1024, 256), BF16),
            pltpu.VMEM((1024, 256), BF16),
            pltpu.VMEM((256, 1024), BF16),
            pltpu.VMEM((8, 1024), F32),
            pltpu.VMEM((8, 1024), F32),
            pltpu.VMEM((2, 4, 2, 4, 16, 1024), BF16),
            pltpu.VMEM((4, 8, 16, 768), F32),
            pltpu.VMEM((4, 2, 16, 768), F32),
            pltpu.VMEM((4, 2, 16, 768), F32),
            pltpu.VMEM((4, 5, 16, 768), F32),
            pltpu.VMEM((4, 8, 16, 768), BF16),
            pltpu.VMEM((4, 8, 2, 8, 1024), F32),
            pltpu.VMEM((4, 8, 8, 1024), F32),
            pltpu.VMEM((3, 4, 2, 16, 512), BF16),
            pltpu.VMEM((4, 2, 16, 512), F32),
            pltpu.VMEM((3, 4, 2, 16, 512), BF16),
            pltpu.VMEM((4, 2, 16, 512), BF16),
            pltpu.VMEM((4, 2, 16, 512), BF16),
            pltpu.VMEM((8, 1024), BF16),
            pltpu.VMEM((1024, 256), BF16),
            pltpu.VMEM((1024, 256), BF16),
            pltpu.VMEM((256, 1024), BF16),
            pltpu.SemaphoreType.DMA((5,)),
            pltpu.SemaphoreType.DMA((4,)),
            pltpu.SemaphoreType.DMA((COPIES,)),
            pltpu.SemaphoreType.DMA((COPIES,)),
        ],
        compiler_params=pltpu.CompilerParams(
            collective_id=0, has_side_effects=True, vmem_limit_bytes=60 << 20),
        cost_estimate=pl.CostEstimate(
            flops=2 * 8 * 512 * 1024 * 256, bytes_accessed=4 << 20, transcendentals=64 * 256),
    )(tokens, out_grad, gate_weight, up_weight, down_weight)
    return pl.pallas_call(
        place,
        out_shape=outs,
        in_specs=[hbm] * 4,
        out_specs=(hbm,) * 4,
        scratch_shapes=[pltpu.SemaphoreType.DMA((4,))],
    )(*results)


def solution(mesh):
    return jax.shard_map(
        per_device,
        mesh=mesh,
        in_specs=(P("gx", "gy"), P("gx", "gy"), P("gy", "gx"), P("gy", "gx"), P("gx", "gy")),
        out_specs=(P("gx", "gy"), P("gy", "gx"), P("gy", "gx"), P("gx", "gy")),
        check_vma=False,
    )
```

```python
import jax
import jax.numpy as jnp
from jax import lax
from jax.experimental import pallas as pl
from jax.experimental.pallas import tpu as pltpu
from jax.sharding import PartitionSpec as P

MESH = pl.DeviceIdType.MESH
BF16, F32 = jnp.bfloat16, jnp.float32

NEAR = (0, 1, -1, 2)
FAR_ORDER = (2, 1, 3)


def dot(a, b, dims):
    return lax.dot_general(a, b, (dims, ((), ())), preferred_element_type=F32)


def kernel(tok_hbm, grad_hbm, gw_hbm, uw_hbm, dw_hbm,
           ig_hbm, gg_hbm, ug_hbm, dg_hbm,
           tok_ref, grad_ref, gw, uw, dw, ex_out, ex_in, x, part, part_low, gate_part, gate_in, b_in, h,
           ig, core_in,
           near_out, near_own, near_in, far_out, far_in,
           ig_ref, gg_ref, ug_ref, dg_ref,
           load_sem, store_sem, send_sem, recv_sem):
    gx, gy = lax.axis_index("gx"), lax.axis_index("gy")
    z, xh, c = gx // 4, (gx // 2) % 2, gx % 2
    y, xl = gy // 2, gy % 2

    def along(dz=0, other_x=False, other_core=False):
        zz = (z + dz + 16) % 16
        xx = 1 - xh if other_x else xh
        cc = 1 - c if other_core else c
        return (zz * 4 + xx * 2 + cc, gy)

    peers = [(dy, dx) for dy in (2, 1, 3, 0) for dx in (1, 0) if dy or dx]

    def across(dy, dx):
        return ((y + dy) % 4) * 2 + (xl + dx) % 2

    loads = [pltpu.make_async_copy(s, d, load_sem.at[i]) for i, (s, d) in enumerate((
        (tok_hbm, tok_ref), (grad_hbm, grad_ref), (gw_hbm, gw), (uw_hbm, uw), (dw_hbm, dw)))]
    for cp in loads:
        cp.start()

    barrier = pltpu.get_barrier_semaphore()
    met = [along(dz) for dz in (8, 4, -4, 2, -2, 1, -1)]
    met += [along(dz, other_x=True) for dz in (8, 4, -4, 0)]
    met += [along(other_core=True)]
    met += [(gx, across(dy, dx)) for dy, dx in peers]
    for dev in met:
        pl.semaphore_signal(barrier, inc=1, device_id=dev, device_id_type=MESH)

    loads[0].wait()
    loads[1].wait()
    first = c == 0
    tok, grad = tok_ref[...].astype(F32), grad_ref[...].astype(F32)
    mine = jnp.where(first, tok, grad)
    ex_out[...] = jnp.where(first, grad, tok)
    pl.semaphore_wait(barrier, len(met))

    sent = []

    def push(src, dst, dev):
        k = len(sent)
        cp = pltpu.make_async_remote_copy(
            src_ref=src, dst_ref=dst, send_sem=send_sem.at[k], recv_sem=recv_sem.at[k],
            device_id=dev, device_id_type=MESH)
        cp.start()
        sent.append(cp)
        return cp

    sibling = along(other_core=True)
    partner = along(other_x=True)

    push(ex_out, ex_in, sibling).wait_recv()
    theirs = ex_in[...]
    block = jnp.concatenate(
        [jnp.where(first, mine, theirs), jnp.where(first, theirs, mine)], axis=0)
    x[c, 0, 0, 0] = block.astype(BF16)

    far = [push(x.at[c, 0, 0, 0], x.at[c, 0, 0, 4 - i], along(4 * i)) for i in FAR_ORDER]
    for cp in far:
        cp.wait_recv()
    whole, low, high = pl.ds(0, 4), pl.ds(0, 2), pl.ds(2, 2)

    def share(n, fs):
        ours = x.at[c, 0, n, fs]
        return push(ours, ours, sibling), push(ours, x.at[c, 1, n, fs], partner), fs, n

    near = [(3, low, push(x.at[c, 0, 0, pl.ds(1, 2)], x.at[c, 0, 3, low], along(2))),
            (3, high, push(x.at[c, 0, 0, high], x.at[c, 0, 3, high], along(-2)))]
    near = [(n, whole, push(x.at[c, 0, 0], x.at[c, 0, n], along(-NEAR[n]))) for n in (1, 2)] + near
    shared = [share(0, whole)]
    for n, fs, cp in near:
        cp.wait_recv()
        shared.append(share(n, fs))

    def products(k):
        rows = x[0, k].reshape(256, 1024)
        up = dot(rows, uw[...], ((1,), (0,))).reshape(8, 32, 256)
        hgrad = dot(x[1, k].reshape(256, 1024), dw[...], ((1,), (1,))).reshape(8, 32, 256)
        part_low[k, :, :, 0:256] = up.astype(BF16)
        part_low[k, :, :, 256:512] = hgrad.astype(BF16)
        part[k, :, :, 0:256] = up
        part[k, :, :, 256:512] = hgrad
        sums = [push(part_low.at[k, across(dy, dx)], b_in.at[k, s], (gx, across(dy, dx)))
                for s, (dy, dx) in enumerate(peers)]
        gate = dot(rows, gw[...], ((1,), (0,))).reshape(8, 32, 256)
        gate_part[k] = gate
        return sums + [push(gate_part.at[k, across(dy, dx)], gate_in.at[k, s], (gx, across(dy, dx)))
                       for s, (dy, dx) in enumerate(peers)]

    def pointwise(k, arrived):
        for cp in arrived:
            cp.wait_recv()
        total, gate = part[k, gy], gate_part[k, gy]
        for s in range(7):
            total = total + b_in[k, s].astype(F32)
            gate = gate + gate_in[k, s]
        up, hgrad = total[:, 0:256], total[:, 256:512]
        sigma = jax.nn.sigmoid(gate)
        act = gate * sigma
        h[k, gy, :, 0:256] = (act * up).astype(BF16)
        h[k, gy, :, 256:512] = (hgrad * up * sigma * (1.0 + gate * (1.0 - sigma))).astype(BF16)
        h[k, gy, :, 512:768] = (hgrad * act).astype(BF16)
        return [push(h.at[k, gy], h.at[k, gy], (gx, across(dy, dx))) for dy, dx in peers]

    def input_products(k, arrived):
        for cp in arrived:
            cp.wait_recv()
        hh = h[k].reshape(256, 768)
        for j in range(2):
            cols = slice(512 * j, 512 * j + 512)
            v = dot(hh[:, 256:512], gw[cols, :], ((1,), (1,)))
            v = v + dot(hh[:, 512:768], uw[cols, :], ((1,), (1,)))
            ig[k, :, :, :, cols] = v.reshape(16, 2, 8, 512)
        return push(ig.at[k, :, 1 - c], core_in.at[k], sibling)

    def send_near(k, arrived):
        arrived.wait_recv()
        for n in range(4):
            for f in range(4):
                s = 4 * n + f
                v = ig[k, s, c] + core_in[k, s]
                v = jnp.concatenate([v[:, 0:512], v[:, 512:1024]], axis=0)
                if n == 0:
                    near_own[k, f] = v
                else:
                    near_out[k, n, f] = v.astype(BF16)
        two = [push(near_out.at[k, 3, fs], near_in.at[k, 3, fs], along(dz))
               for fs, dz in ((low, 2), (high, -2))]
        return two + [push(near_out.at[k, n], near_in.at[k, n], along(NEAR[n])) for n in (1, 2)]

    def send_far(k, arrived):
        for cp in arrived:
            cp.wait_recv()
        for f in range(4):
            v = near_own[k, f]
            for n in (1, 2):
                v = v + near_in[k, n, f].astype(F32)
            if f < 2:
                v = v + near_in[k, 3, f].astype(F32)
            if f in (0, 3):
                v = v + near_in[k, 3, (f + 3) % 4].astype(F32)
            if k == 0 and f == 0:
                near_own[k, f] = v
            else:
                far_out[k, f] = v.astype(BF16)
        order = FAR_ORDER if k == 0 else FAR_ORDER + (0,)
        return [push(far_out.at[k, f], far_in.at[k, f], along(4 * f, other_x=k == 1))
                for f in order]

    for cp in loads[2:]:
        cp.wait()
    for from_core, _, _, _ in shared:
        from_core.wait_recv()
    b0 = products(0)

    to_core = []
    for _, from_x, fs, n in shared:
        from_x.wait_recv()
        other = x.at[c, 1, n, fs]
        to_core.append(push(other, other, sibling))
    for cp in to_core:
        cp.wait_recv()
    b1 = products(1)

    c0 = pointwise(0, b0)
    c1 = pointwise(1, b1)
    i0 = input_products(0, c0)
    n0 = send_near(0, i0)
    i1 = input_products(1, c1)
    n1 = send_near(1, i1)
    f0 = send_far(0, n0)
    f1 = send_far(1, n1)

    factor = 1.0 / jnp.sqrt(F32(512))

    @pl.loop(0, 4)
    def _(i):
        cols = pl.ds(pl.multiple_of(i * 256, 256), 256)
        hh = h[...].reshape(512, 768)
        t = x[0, :, :, :, :, cols].reshape(512, 256)
        gg_ref[cols, :] = (dot(t, hh[:, 256:512], ((0,), (0,))) * factor).astype(BF16)
        ug_ref[cols, :] = (dot(t, hh[:, 512:768], ((0,), (0,))) * factor).astype(BF16)
        g = x[1, :, :, :, :, cols].reshape(512, 256)
        dg_ref[:, cols] = (dot(hh[:, 0:256], g, ((0,), (0,))) * factor).astype(BF16)

    stores = [pltpu.make_async_copy(s, d, store_sem.at[i]) for i, (s, d) in enumerate((
        (gg_ref, gg_hbm), (ug_ref, ug_hbm), (dg_ref, dg_hbm), (ig_ref, ig_hbm)))]
    for cp in stores[:3]:
        cp.start()
    for cp in f0 + f1:
        cp.wait_recv()
    v = near_own[0, 0] + far_in[1, 0].astype(F32)
    for f in (1, 2, 3):
        v = v + (far_in[0, f].astype(F32) + far_in[1, f].astype(F32))
    ig_ref[...] = jnp.concatenate([v[0:8], v[8:16]], axis=1).astype(BF16)

    stores[3].start()
    for cp in sent:
        cp.wait_send()
    for cp in stores:
        cp.wait()


COPIES = 86


def place(*refs):
    given, wanted, held, load_sem, store_sem = refs[:4], refs[4:8], refs[8:12], refs[12], refs[13]
    loads = [pltpu.make_async_copy(s, v, load_sem.at[i])
             for i, (s, v) in enumerate(zip(given, held))]
    stores = [pltpu.make_async_copy(v, d, store_sem.at[i])
              for i, (v, d) in enumerate(zip(held, wanted))]
    for cp in loads:
        cp.start()
    for load, store in zip(loads, stores):
        load.wait()
        store.start()
    for cp in stores:
        cp.wait()


def per_device(tokens, out_grad, gate_weight, up_weight, down_weight):
    hbm = pl.BlockSpec(memory_space=pl.ANY)
    shape = jax.ShapeDtypeStruct
    outs = (shape((8, 1024), BF16), shape((1024, 256), BF16),
            shape((1024, 256), BF16), shape((256, 1024), BF16))
    results = pl.pallas_call(
        kernel,
        out_shape=outs,
        in_specs=[hbm] * 5,
        out_specs=(hbm,) * 4,
        scratch_shapes=[
            pltpu.VMEM((8, 1024), BF16),
            pltpu.VMEM((8, 1024), BF16),
            pltpu.VMEM((1024, 256), BF16),
            pltpu.VMEM((1024, 256), BF16),
            pltpu.VMEM((256, 1024), BF16),
            pltpu.VMEM((8, 1024), F32),
            pltpu.VMEM((8, 1024), F32),
            pltpu.VMEM((2, 2, 4, 4, 16, 1024), BF16),
            pltpu.VMEM((2, 8, 32, 512), F32),
            pltpu.VMEM((2, 8, 32, 512), BF16),
            pltpu.VMEM((2, 8, 32, 256), F32),
            pltpu.VMEM((2, 7, 32, 256), F32),
            pltpu.VMEM((2, 7, 32, 512), BF16),
            pltpu.VMEM((2, 8, 32, 768), BF16),
            pltpu.VMEM((2, 16, 2, 8, 1024), F32),
            pltpu.VMEM((2, 16, 8, 1024), F32),
            pltpu.VMEM((2, 4, 4, 16, 512), BF16),
            pltpu.VMEM((2, 4, 16, 512), F32),
            pltpu.VMEM((2, 4, 4, 16, 512), BF16),
            pltpu.VMEM((2, 4, 16, 512), BF16),
            pltpu.VMEM((2, 4, 16, 512), BF16),
            pltpu.VMEM((8, 1024), BF16),
            pltpu.VMEM((1024, 256), BF16),
            pltpu.VMEM((1024, 256), BF16),
            pltpu.VMEM((256, 1024), BF16),
            pltpu.SemaphoreType.DMA((5,)),
            pltpu.SemaphoreType.DMA((4,)),
            pltpu.SemaphoreType.DMA((COPIES,)),
            pltpu.SemaphoreType.DMA((COPIES,)),
        ],
        compiler_params=pltpu.CompilerParams(
            collective_id=0, has_side_effects=True, vmem_limit_bytes=60 << 20),
        cost_estimate=pl.CostEstimate(
            flops=2 * 8 * 512 * 1024 * 256, bytes_accessed=4 << 20, transcendentals=64 * 256),
    )(tokens, out_grad, gate_weight, up_weight, down_weight)
    return pl.pallas_call(
        place,
        out_shape=outs,
        in_specs=[hbm] * 4,
        out_specs=(hbm,) * 4,
        scratch_shapes=[pltpu.VMEM(o.shape, BF16) for o in outs]
        + [pltpu.SemaphoreType.DMA((4,))] * 2,
        compiler_params=pltpu.CompilerParams(vmem_limit_bytes=60 << 20),
    )(*results)


def solution(mesh):
    return jax.shard_map(
        per_device,
        mesh=mesh,
        in_specs=(P("gx", "gy"), P("gx", "gy"), P("gy", "gx"), P("gy", "gx"), P("gx", "gy")),
        out_specs=(P("gx", "gy"), P("gy", "gx"), P("gy", "gx"), P("gx", "gy")),
        check_vma=False,
    )
```

```python
import jax
import jax.numpy as jnp
from jax import lax
from jax.experimental import pallas as pl
from jax.experimental.pallas import tpu as pltpu
from jax.sharding import PartitionSpec as P

MESH = pl.DeviceIdType.MESH
BF16, F32 = jnp.bfloat16, jnp.float32

NEAR = (0, 1, -1, 2)
FAR_ORDER = (2, 1, 3)
PLACE = (1, 2, 0, 3)


def dot(a, b, dims):
    return lax.dot_general(a, b, (dims, ((), ())), preferred_element_type=F32)


def kernel(tok_hbm, grad_hbm, gw_hbm, uw_hbm, dw_hbm,
           ig_hbm, gg_hbm, ug_hbm, dg_hbm,
           tok_ref, grad_ref, gw, uw, dw, ex_out, ex_in, x, part, part_low, gate_part, gate_in, b_in, h,
           ig, core_in,
           near_out, near_own, near_in, far_out, far_in,
           ig_ref, gg_ref, ug_ref, dg_ref,
           load_sem, store_sem, send_sem, recv_sem):
    gx, gy = lax.axis_index("gx"), lax.axis_index("gy")
    z, xh, c = gx // 4, (gx // 2) % 2, gx % 2
    y, xl = gy // 2, gy % 2

    def along(dz=0, other_x=False, other_core=False):
        zz = (z + dz + 16) % 16
        xx = 1 - xh if other_x else xh
        cc = 1 - c if other_core else c
        return (zz * 4 + xx * 2 + cc, gy)

    peers = [(dy, dx) for dy in (2, 1, 3, 0) for dx in (1, 0) if dy or dx]

    def across(dy, dx):
        return ((y + dy) % 4) * 2 + (xl + dx) % 2

    loads = [pltpu.make_async_copy(s, d, load_sem.at[i]) for i, (s, d) in enumerate((
        (tok_hbm, tok_ref), (grad_hbm, grad_ref), (gw_hbm, gw), (uw_hbm, uw), (dw_hbm, dw)))]
    for cp in loads:
        cp.start()

    barrier = pltpu.get_barrier_semaphore()
    met = [along(dz) for dz in (8, 4, -4, 2, -2, 1, -1)]
    met += [along(dz, other_x=True) for dz in (8, 4, -4, 0)]
    met += [along(other_core=True)]
    met += [(gx, across(dy, dx)) for dy, dx in peers]
    for dev in met:
        pl.semaphore_signal(barrier, inc=1, device_id=dev, device_id_type=MESH)

    loads[0].wait()
    loads[1].wait()
    first = c == 0
    tok, grad = tok_ref[...].astype(F32), grad_ref[...].astype(F32)
    mine = jnp.where(first, tok, grad)
    ex_out[...] = jnp.where(first, grad, tok)
    pl.semaphore_wait(barrier, len(met))

    sent = []

    def push(src, dst, dev):
        k = len(sent)
        cp = pltpu.make_async_remote_copy(
            src_ref=src, dst_ref=dst, send_sem=send_sem.at[k], recv_sem=recv_sem.at[k],
            device_id=dev, device_id_type=MESH)
        cp.start()
        sent.append(cp)
        return cp

    sibling = along(other_core=True)
    partner = along(other_x=True)

    push(ex_out, ex_in, sibling).wait_recv()
    theirs = ex_in[...]
    block = jnp.concatenate(
        [jnp.where(first, mine, theirs), jnp.where(first, theirs, mine)], axis=0)
    x[c, 0, 0, 0] = block.astype(BF16)

    shared, arriving = [], {}

    def share(n, f):
        ours = x.at[c, 0, n, f]
        from_x = push(ours, x.at[c, 1, n, f], partner)
        shared.append((push(ours, ours, sibling), from_x, n, f))

    def to_near(f):
        ours = x.at[c, 0, 0, f]
        if f < 2:
            arriving[3, f] = push(ours, x.at[c, 0, 3, f], along(-2))
        if f in (0, 3):
            arriving[3, (f + 3) % 4] = push(ours, x.at[c, 0, 3, (f + 3) % 4], along(2))
        for n in (1, 2):
            arriving[n, f] = push(ours, x.at[c, 0, n, f], along(-NEAR[n]))

    def pass_on(*slots):
        for slot in slots:
            arriving.pop(slot).wait_recv()
            share(*slot)

    for i in FAR_ORDER:
        arriving[0, 4 - i] = push(x.at[c, 0, 0, 0], x.at[c, 0, 0, 4 - i], along(4 * i))
    to_near(0)
    share(0, 0)
    pass_on((1, 0), (2, 0), (3, 0), (3, 3))
    for f in (1, 3, 2):
        arriving.pop((0, f)).wait_recv()
        to_near(f)
        share(0, f)
    pass_on((1, 1), (2, 1), (3, 1), (1, 3), (2, 3), (3, 2), (1, 2), (2, 2))

    def products(k):
        rows = x[0, k].reshape(256, 1024)
        up = dot(rows, uw[...], ((1,), (0,))).reshape(8, 32, 256)
        hgrad = dot(x[1, k].reshape(256, 1024), dw[...], ((1,), (1,))).reshape(8, 32, 256)
        part_low[k, :, :, 0:256] = up.astype(BF16)
        part_low[k, :, :, 256:512] = hgrad.astype(BF16)
        part[k, :, :, 0:256] = up
        part[k, :, :, 256:512] = hgrad
        sums = [push(part_low.at[k, across(dy, dx)], b_in.at[k, s], (gx, across(dy, dx)))
                for s, (dy, dx) in enumerate(peers)]
        gate = dot(rows, gw[...], ((1,), (0,))).reshape(8, 32, 256)
        gate_part[k] = gate
        return sums + [push(gate_part.at[k, across(dy, dx)], gate_in.at[k, s], (gx, across(dy, dx)))
                       for s, (dy, dx) in enumerate(peers)]

    def pointwise(k, arrived):
        for cp in arrived:
            cp.wait_recv()
        total, gate = part[k, gy], gate_part[k, gy]
        for s in range(7):
            total = total + b_in[k, s].astype(F32)
            gate = gate + gate_in[k, s]
        up, hgrad = total[:, 0:256], total[:, 256:512]
        sigma = jax.nn.sigmoid(gate)
        act = gate * sigma
        h[k, gy, :, 0:256] = (act * up).astype(BF16)
        h[k, gy, :, 256:512] = (hgrad * up * sigma * (1.0 + gate * (1.0 - sigma))).astype(BF16)
        h[k, gy, :, 512:768] = (hgrad * act).astype(BF16)
        return [push(h.at[k, gy], h.at[k, gy], (gx, across(dy, dx))) for dy, dx in peers]

    def input_products(k, arrived):
        for cp in arrived:
            cp.wait_recv()
        hh = h[k].reshape(256, 768)
        for j in range(2):
            cols = slice(512 * j, 512 * j + 512)
            v = dot(hh[:, 256:512], gw[cols, :], ((1,), (1,)))
            v = v + dot(hh[:, 512:768], uw[cols, :], ((1,), (1,)))
            ig[k, :, :, :, cols] = v.reshape(16, 2, 8, 512)
        return push(ig.at[k, :, 1 - c], core_in.at[k], sibling)

    def send_near(k, arrived):
        arrived.wait_recv()
        for n in range(4):
            for f in range(4):
                s = 4 * n + f
                v = ig[k, s, c] + core_in[k, s]
                v = jnp.concatenate([v[:, 0:512], v[:, 512:1024]], axis=0)
                if n == 0:
                    near_own[k, f] = v
                else:
                    near_out[k, n, f if n == 3 else PLACE[f]] = v.astype(BF16)

        def to(n, fs, dz):
            return push(near_out.at[k, n, fs], near_in.at[k, n, fs], along(dz))

        early = [to(n, pl.ds(0, 1), NEAR[n]) for n in (1, 2)]
        late = [to(3, pl.ds(0, 2), 2), to(3, pl.ds(2, 2), -2)]
        return early, late + [to(n, pl.ds(1, 3), NEAR[n]) for n in (1, 2)]

    def send_far(k, early, late):
        out = []
        for cp in early:
            cp.wait_recv()
        for f in FAR_ORDER + (0,):
            if f == FAR_ORDER[1]:
                for cp in late:
                    cp.wait_recv()
            v = near_own[k, f]
            for n in (1, 2):
                v = v + near_in[k, n, PLACE[f]].astype(F32)
            if f < 2:
                v = v + near_in[k, 3, f].astype(F32)
            if f in (0, 3):
                v = v + near_in[k, 3, (f + 3) % 4].astype(F32)
            if k == 0 and f == 0:
                near_own[k, f] = v
            else:
                far_out[k, f] = v.astype(BF16)
                out.append(push(far_out.at[k, f], far_in.at[k, f],
                                along(4 * f, other_x=k == 1)))
        return out

    for cp in loads[2:]:
        cp.wait()
    for from_core, _, _, _ in shared:
        from_core.wait_recv()
    b0 = products(0)

    to_core = []
    for _, from_x, n, f in shared:
        from_x.wait_recv()
        other = x.at[c, 1, n, f]
        to_core.append(push(other, other, sibling))
    for cp in to_core:
        cp.wait_recv()
    b1 = products(1)

    c0 = pointwise(0, b0)
    c1 = pointwise(1, b1)
    i0 = input_products(0, c0)
    n0 = send_near(0, i0)
    i1 = input_products(1, c1)
    n1 = send_near(1, i1)
    f0 = send_far(0, *n0)
    f1 = send_far(1, *n1)

    factor = 1.0 / jnp.sqrt(F32(512))

    @pl.loop(0, 4)
    def _(i):
        cols = pl.ds(pl.multiple_of(i * 256, 256), 256)
        hh = h[...].reshape(512, 768)
        t = x[0, :, :, :, :, cols].reshape(512, 256)
        gg_ref[cols, :] = (dot(t, hh[:, 256:512], ((0,), (0,))) * factor).astype(BF16)
        ug_ref[cols, :] = (dot(t, hh[:, 512:768], ((0,), (0,))) * factor).astype(BF16)
        g = x[1, :, :, :, :, cols].reshape(512, 256)
        dg_ref[:, cols] = (dot(hh[:, 0:256], g, ((0,), (0,))) * factor).astype(BF16)

    stores = [pltpu.make_async_copy(s, d, store_sem.at[i]) for i, (s, d) in enumerate((
        (gg_ref, gg_hbm), (ug_ref, ug_hbm), (dg_ref, dg_hbm), (ig_ref, ig_hbm)))]
    for cp in stores[:3]:
        cp.start()
    for cp in f0 + f1:
        cp.wait_recv()
    v = near_own[0, 0] + far_in[1, 0].astype(F32)
    for f in (1, 2, 3):
        v = v + (far_in[0, f].astype(F32) + far_in[1, f].astype(F32))
    ig_ref[...] = jnp.concatenate([v[0:8], v[8:16]], axis=1).astype(BF16)

    stores[3].start()
    for cp in sent:
        cp.wait_send()
    for cp in stores:
        cp.wait()


COPIES = 128


def place(*refs):
    given, wanted, held, load_sem, store_sem = refs[:4], refs[4:8], refs[8:12], refs[12], refs[13]
    loads = [pltpu.make_async_copy(s, v, load_sem.at[i])
             for i, (s, v) in enumerate(zip(given, held))]
    stores = [pltpu.make_async_copy(v, d, store_sem.at[i])
              for i, (v, d) in enumerate(zip(held, wanted))]
    for cp in loads:
        cp.start()
    for load, store in zip(loads, stores):
        load.wait()
        store.start()
    for cp in stores:
        cp.wait()


def per_device(tokens, out_grad, gate_weight, up_weight, down_weight):
    hbm = pl.BlockSpec(memory_space=pl.ANY)
    shape = jax.ShapeDtypeStruct
    outs = (shape((8, 1024), BF16), shape((1024, 256), BF16),
            shape((1024, 256), BF16), shape((256, 1024), BF16))
    results = pl.pallas_call(
        kernel,
        out_shape=outs,
        in_specs=[hbm] * 5,
        out_specs=(hbm,) * 4,
        scratch_shapes=[
            pltpu.VMEM((8, 1024), BF16),
            pltpu.VMEM((8, 1024), BF16),
            pltpu.VMEM((1024, 256), BF16),
            pltpu.VMEM((1024, 256), BF16),
            pltpu.VMEM((256, 1024), BF16),
            pltpu.VMEM((8, 1024), F32),
            pltpu.VMEM((8, 1024), F32),
            pltpu.VMEM((2, 2, 4, 4, 16, 1024), BF16),
            pltpu.VMEM((2, 8, 32, 512), F32),
            pltpu.VMEM((2, 8, 32, 512), BF16),
            pltpu.VMEM((2, 8, 32, 256), F32),
            pltpu.VMEM((2, 7, 32, 256), F32),
            pltpu.VMEM((2, 7, 32, 512), BF16),
            pltpu.VMEM((2, 8, 32, 768), BF16),
            pltpu.VMEM((2, 16, 2, 8, 1024), F32),
            pltpu.VMEM((2, 16, 8, 1024), F32),
            pltpu.VMEM((2, 4, 4, 16, 512), BF16),
            pltpu.VMEM((2, 4, 16, 512), F32),
            pltpu.VMEM((2, 4, 4, 16, 512), BF16),
            pltpu.VMEM((2, 4, 16, 512), BF16),
            pltpu.VMEM((2, 4, 16, 512), BF16),
            pltpu.VMEM((8, 1024), BF16),
            pltpu.VMEM((1024, 256), BF16),
            pltpu.VMEM((1024, 256), BF16),
            pltpu.VMEM((256, 1024), BF16),
            pltpu.SemaphoreType.DMA((5,)),
            pltpu.SemaphoreType.DMA((4,)),
            pltpu.SemaphoreType.DMA((COPIES,)),
            pltpu.SemaphoreType.DMA((COPIES,)),
        ],
        compiler_params=pltpu.CompilerParams(
            collective_id=0, has_side_effects=True, vmem_limit_bytes=60 << 20),
        cost_estimate=pl.CostEstimate(
            flops=2 * 8 * 512 * 1024 * 256, bytes_accessed=4 << 20, transcendentals=64 * 256),
    )(tokens, out_grad, gate_weight, up_weight, down_weight)
    return pl.pallas_call(
        place,
        out_shape=outs,
        in_specs=[hbm] * 4,
        out_specs=(hbm,) * 4,
        scratch_shapes=[pltpu.VMEM(o.shape, BF16) for o in outs]
        + [pltpu.SemaphoreType.DMA((4,))] * 2,
        compiler_params=pltpu.CompilerParams(vmem_limit_bytes=60 << 20),
    )(*results)


def solution(mesh):
    return jax.shard_map(
        per_device,
        mesh=mesh,
        in_specs=(P("gx", "gy"), P("gx", "gy"), P("gy", "gx"), P("gy", "gx"), P("gx", "gy")),
        out_specs=(P("gx", "gy"), P("gy", "gx"), P("gy", "gx"), P("gx", "gy")),
        check_vma=False,
    )
```

```python
import jax
import jax.numpy as jnp
from jax import lax
from jax.experimental import pallas as pl
from jax.experimental.pallas import tpu as pltpu
from jax.sharding import PartitionSpec as P

MESH = pl.DeviceIdType.MESH
BF16, F32 = jnp.bfloat16, jnp.float32

NEAR = (0, 1, -1, 2)
FAR_ORDER = (2, 1, 3)
PLACE = (1, 2, 0, 3)


def dot(a, b, dims):
    return lax.dot_general(a, b, (dims, ((), ())), preferred_element_type=F32)


def kernel(tok_hbm, grad_hbm, gw_hbm, uw_hbm, dw_hbm,
           ig_hbm, gg_hbm, ug_hbm, dg_hbm,
           tok_ref, grad_ref, gw, uw, dw, ex_out, ex_in, x, part, part_low, gate_part, gate_in, b_in, h, hidden,
           ig, core_in,
           near_out, near_own, near_in, far_out, far_in,
           ig_ref, gg_ref, ug_ref, dg_ref,
           load_sem, store_sem, send_sem, recv_sem):
    gx, gy = lax.axis_index("gx"), lax.axis_index("gy")
    z, xh, c = gx // 4, (gx // 2) % 2, gx % 2
    y, xl = gy // 2, gy % 2

    def along(dz=0, other_x=False, other_core=False):
        zz = (z + dz + 16) % 16
        xx = 1 - xh if other_x else xh
        cc = 1 - c if other_core else c
        return (zz * 4 + xx * 2 + cc, gy)

    peers = [(dy, dx) for dy in (2, 1, 3, 0) for dx in (1, 0) if dy or dx]

    def across(dy, dx):
        return ((y + dy) % 4) * 2 + (xl + dx) % 2

    loads = [pltpu.make_async_copy(s, d, load_sem.at[i]) for i, (s, d) in enumerate((
        (tok_hbm, tok_ref), (grad_hbm, grad_ref), (gw_hbm, gw), (uw_hbm, uw), (dw_hbm, dw)))]
    for cp in loads:
        cp.start()

    barrier = pltpu.get_barrier_semaphore()
    met = [along(dz) for dz in (8, 4, -4, 2, -2, 1, -1)]
    met += [along(dz, other_x=True) for dz in (8, 4, -4, 0)]
    met += [along(other_core=True)]
    met += [(gx, across(dy, dx)) for dy, dx in peers]
    for dev in met:
        pl.semaphore_signal(barrier, inc=1, device_id=dev, device_id_type=MESH)

    loads[0].wait()
    loads[1].wait()
    first = c == 0
    tok, grad = tok_ref[...].astype(F32), grad_ref[...].astype(F32)
    mine = jnp.where(first, tok, grad)
    ex_out[...] = jnp.where(first, grad, tok)
    pl.semaphore_wait(barrier, len(met))

    sent = []

    def push(src, dst, dev):
        k = len(sent)
        cp = pltpu.make_async_remote_copy(
            src_ref=src, dst_ref=dst, send_sem=send_sem.at[k], recv_sem=recv_sem.at[k],
            device_id=dev, device_id_type=MESH)
        cp.start()
        sent.append(cp)
        return cp

    sibling = along(other_core=True)
    partner = along(other_x=True)

    push(ex_out, ex_in, sibling).wait_recv()
    theirs = ex_in[...]
    block = jnp.concatenate(
        [jnp.where(first, mine, theirs), jnp.where(first, theirs, mine)], axis=0)
    x[c, 0, 0, 0] = block.astype(BF16)

    shared, arriving = [], {}

    def share(n, f):
        ours = x.at[c, 0, n, f]
        from_x = push(ours, x.at[c, 1, n, f], partner)
        shared.append((push(ours, ours, sibling), from_x, n, f))

    def to_near(f):
        ours = x.at[c, 0, 0, f]
        if f < 2:
            arriving[3, f] = push(ours, x.at[c, 0, 3, f], along(-2))
        if f in (0, 3):
            arriving[3, (f + 3) % 4] = push(ours, x.at[c, 0, 3, (f + 3) % 4], along(2))
        for n in (1, 2):
            arriving[n, f] = push(ours, x.at[c, 0, n, f], along(-NEAR[n]))

    def pass_on(*slots):
        for slot in slots:
            arriving.pop(slot).wait_recv()
            share(*slot)

    for i in FAR_ORDER:
        arriving[0, 4 - i] = push(x.at[c, 0, 0, 0], x.at[c, 0, 0, 4 - i], along(4 * i))
    to_near(0)
    share(0, 0)
    pass_on((1, 0), (2, 0), (3, 0), (3, 3))
    for f in (1, 3, 2):
        arriving.pop((0, f)).wait_recv()
        to_near(f)
        share(0, f)
    pass_on((1, 1), (2, 1), (3, 1), (1, 3), (2, 3), (3, 2), (1, 2), (2, 2))

    def products(k):
        rows = x[0, k].reshape(256, 1024)
        up = dot(rows, uw[...], ((1,), (0,))).reshape(8, 32, 256)
        hgrad = dot(x[1, k].reshape(256, 1024), dw[...], ((1,), (1,))).reshape(8, 32, 256)
        part_low[k, :, :, 0:256] = up.astype(BF16)
        part_low[k, :, :, 256:512] = hgrad.astype(BF16)
        part[k, :, :, 0:256] = up
        part[k, :, :, 256:512] = hgrad
        sums = [push(part_low.at[k, across(dy, dx)], b_in.at[k, s], (gx, across(dy, dx)))
                for s, (dy, dx) in enumerate(peers)]
        gate = dot(rows, gw[...], ((1,), (0,))).reshape(8, 32, 256)
        gate_part[k] = gate
        return sums + [push(gate_part.at[k, across(dy, dx)], gate_in.at[k, s], (gx, across(dy, dx)))
                       for s, (dy, dx) in enumerate(peers)]

    def pointwise(k, arrived):
        for cp in arrived:
            cp.wait_recv()
        total, gate = part[k, gy], gate_part[k, gy]
        for s in range(7):
            total = total + b_in[k, s].astype(F32)
            gate = gate + gate_in[k, s]
        up, hgrad = total[:, 0:256], total[:, 256:512]
        sigma = jax.nn.sigmoid(gate)
        act = gate * sigma
        h[k, gy, :, 0:256] = (hgrad * up * sigma * (1.0 + gate * (1.0 - sigma))).astype(BF16)
        h[k, gy, :, 256:512] = (hgrad * act).astype(BF16)
        hidden[k, gy] = (act * up).astype(BF16)
        return spread(k, h)

    def spread(k, ref):
        return [push(ref.at[k, gy], ref.at[k, gy], (gx, across(dy, dx))) for dy, dx in peers]

    def input_products(k, arrived):
        for cp in arrived:
            cp.wait_recv()
        hh = h[k].reshape(256, 512)
        for j in range(2):
            cols = slice(512 * j, 512 * j + 512)
            v = dot(hh[:, 0:256], gw[cols, :], ((1,), (1,)))
            v = v + dot(hh[:, 256:512], uw[cols, :], ((1,), (1,)))
            ig[k, :, :, :, cols] = v.reshape(16, 2, 8, 512)
        return push(ig.at[k, :, 1 - c], core_in.at[k], sibling)

    def send_near(k, arrived):
        arrived.wait_recv()
        for n in range(4):
            for f in range(4):
                s = 4 * n + f
                v = ig[k, s, c] + core_in[k, s]
                v = jnp.concatenate([v[:, 0:512], v[:, 512:1024]], axis=0)
                if n == 0:
                    near_own[k, f] = v
                else:
                    near_out[k, n, f if n == 3 else PLACE[f]] = v.astype(BF16)

        def to(n, fs, dz):
            return push(near_out.at[k, n, fs], near_in.at[k, n, fs], along(dz))

        early = [to(n, pl.ds(0, 1), NEAR[n]) for n in (1, 2)]
        late = [to(3, pl.ds(0, 2), 2), to(3, pl.ds(2, 2), -2)]
        return early, late + [to(n, pl.ds(1, 3), NEAR[n]) for n in (1, 2)]

    def send_far(k, early, late):
        out = []
        for cp in early:
            cp.wait_recv()
        for f in FAR_ORDER + (0,):
            if f == FAR_ORDER[1]:
                for cp in late:
                    cp.wait_recv()
            v = near_own[k, f]
            for n in (1, 2):
                v = v + near_in[k, n, PLACE[f]].astype(F32)
            if f < 2:
                v = v + near_in[k, 3, f].astype(F32)
            if f in (0, 3):
                v = v + near_in[k, 3, (f + 3) % 4].astype(F32)
            if k == 0 and f == 0:
                near_own[k, f] = v
            else:
                far_out[k, f] = v.astype(BF16)
                out.append(push(far_out.at[k, f], far_in.at[k, f],
                                along(4 * f, other_x=k == 1)))
        return out

    for cp in loads[2:]:
        cp.wait()
    for from_core, _, _, _ in shared:
        from_core.wait_recv()
    b0 = products(0)

    to_core = []
    for _, from_x, n, f in shared:
        from_x.wait_recv()
        other = x.at[c, 1, n, f]
        to_core.append(push(other, other, sibling))
    for cp in to_core:
        cp.wait_recv()
    b1 = products(1)

    c0 = pointwise(0, b0)
    c1 = pointwise(1, b1)
    i0 = input_products(0, c0)
    n0 = send_near(0, i0)
    spread_hidden = spread(0, hidden)
    i1 = input_products(1, c1)
    n1 = send_near(1, i1)
    spread_hidden += spread(1, hidden)
    f0 = send_far(0, *n0)
    f1 = send_far(1, *n1)

    for cp in spread_hidden:
        cp.wait_recv()
    factor = 1.0 / jnp.sqrt(F32(512))

    @pl.loop(0, 4)
    def _(i):
        cols = pl.ds(pl.multiple_of(i * 256, 256), 256)
        hh = h[...].reshape(512, 512)
        t = x[0, :, :, :, :, cols].reshape(512, 256)
        gg_ref[cols, :] = (dot(t, hh[:, 0:256], ((0,), (0,))) * factor).astype(BF16)
        ug_ref[cols, :] = (dot(t, hh[:, 256:512], ((0,), (0,))) * factor).astype(BF16)
        g = x[1, :, :, :, :, cols].reshape(512, 256)
        dg_ref[:, cols] = (dot(
            hidden[...].reshape(512, 256), g, ((0,), (0,))) * factor).astype(BF16)

    stores = [pltpu.make_async_copy(s, d, store_sem.at[i]) for i, (s, d) in enumerate((
        (gg_ref, gg_hbm), (ug_ref, ug_hbm), (dg_ref, dg_hbm), (ig_ref, ig_hbm)))]
    for cp in stores[:3]:
        cp.start()
    for cp in sent:
        cp.wait_send()
    for cp in f0 + f1:
        cp.wait_recv()
    v = near_own[0, 0] + far_in[1, 0].astype(F32)
    for f in (1, 2, 3):
        v = v + (far_in[0, f].astype(F32) + far_in[1, f].astype(F32))
    ig_ref[...] = jnp.concatenate([v[0:8], v[8:16]], axis=1).astype(BF16)

    stores[3].start()
    for cp in stores:
        cp.wait()


COPIES = 144


def place(*refs):
    given, wanted, held, load_sem, store_sem = refs[:4], refs[4:8], refs[8:12], refs[12], refs[13]
    loads = [pltpu.make_async_copy(s, v, load_sem.at[i])
             for i, (s, v) in enumerate(zip(given, held))]
    stores = [pltpu.make_async_copy(v, d, store_sem.at[i])
              for i, (v, d) in enumerate(zip(held, wanted))]
    for cp in loads:
        cp.start()
    for load, store in zip(loads, stores):
        load.wait()
        store.start()
    for cp in stores:
        cp.wait()


def per_device(tokens, out_grad, gate_weight, up_weight, down_weight):
    hbm = pl.BlockSpec(memory_space=pl.ANY)
    shape = jax.ShapeDtypeStruct
    outs = (shape((8, 1024), BF16), shape((1024, 256), BF16),
            shape((1024, 256), BF16), shape((256, 1024), BF16))
    results = pl.pallas_call(
        kernel,
        out_shape=outs,
        in_specs=[hbm] * 5,
        out_specs=(hbm,) * 4,
        scratch_shapes=[
            pltpu.VMEM((8, 1024), BF16),
            pltpu.VMEM((8, 1024), BF16),
            pltpu.VMEM((1024, 256), BF16),
            pltpu.VMEM((1024, 256), BF16),
            pltpu.VMEM((256, 1024), BF16),
            pltpu.VMEM((8, 1024), F32),
            pltpu.VMEM((8, 1024), F32),
            pltpu.VMEM((2, 2, 4, 4, 16, 1024), BF16),
            pltpu.VMEM((2, 8, 32, 512), F32),
            pltpu.VMEM((2, 8, 32, 512), BF16),
            pltpu.VMEM((2, 8, 32, 256), F32),
            pltpu.VMEM((2, 7, 32, 256), F32),
            pltpu.VMEM((2, 7, 32, 512), BF16),
            pltpu.VMEM((2, 8, 32, 512), BF16),
            pltpu.VMEM((2, 8, 32, 256), BF16),
            pltpu.VMEM((2, 16, 2, 8, 1024), F32),
            pltpu.VMEM((2, 16, 8, 1024), F32),
            pltpu.VMEM((2, 4, 4, 16, 512), BF16),
            pltpu.VMEM((2, 4, 16, 512), F32),
            pltpu.VMEM((2, 4, 4, 16, 512), BF16),
            pltpu.VMEM((2, 4, 16, 512), BF16),
            pltpu.VMEM((2, 4, 16, 512), BF16),
            pltpu.VMEM((8, 1024), BF16),
            pltpu.VMEM((1024, 256), BF16),
            pltpu.VMEM((1024, 256), BF16),
            pltpu.VMEM((256, 1024), BF16),
            pltpu.SemaphoreType.DMA((5,)),
            pltpu.SemaphoreType.DMA((4,)),
            pltpu.SemaphoreType.DMA((COPIES,)),
            pltpu.SemaphoreType.DMA((COPIES,)),
        ],
        compiler_params=pltpu.CompilerParams(
            collective_id=0, has_side_effects=True, vmem_limit_bytes=60 << 20),
        cost_estimate=pl.CostEstimate(
            flops=2 * 8 * 512 * 1024 * 256, bytes_accessed=4 << 20, transcendentals=64 * 256),
    )(tokens, out_grad, gate_weight, up_weight, down_weight)
    return pl.pallas_call(
        place,
        out_shape=outs,
        in_specs=[hbm] * 4,
        out_specs=(hbm,) * 4,
        scratch_shapes=[pltpu.VMEM(o.shape, BF16) for o in outs]
        + [pltpu.SemaphoreType.DMA((4,))] * 2,
        compiler_params=pltpu.CompilerParams(vmem_limit_bytes=60 << 20),
    )(*results)


def solution(mesh):
    return jax.shard_map(
        per_device,
        mesh=mesh,
        in_specs=(P("gx", "gy"), P("gx", "gy"), P("gy", "gx"), P("gy", "gx"), P("gx", "gy")),
        out_specs=(P("gx", "gy"), P("gy", "gx"), P("gy", "gx"), P("gx", "gy")),
        check_vma=False,
    )
```

```python
import jax
import jax.numpy as jnp
from jax import lax
from jax.experimental import pallas as pl
from jax.experimental.pallas import tpu as pltpu
from jax.sharding import PartitionSpec as P

MESH = pl.DeviceIdType.MESH
BF16, F32 = jnp.bfloat16, jnp.float32

NEAR = (0, 1, -1, 2)
FAR_ORDER = (2, 1, 3)
PLACE = (1, 2, 0, 3)


def dot(a, b, dims):
    return lax.dot_general(a, b, (dims, ((), ())), preferred_element_type=F32)


def kernel(tok_hbm, grad_hbm, gw_hbm, uw_hbm, dw_hbm,
           ig_hbm, gg_hbm, ug_hbm, dg_hbm,
           tok_ref, grad_ref, gw, uw, dw, ex_out, ex_in, x, part, part_low, b_in, h, hidden,
           ig, core_in,
           near_out, near_own, near_in, far_out, far_in,
           ig_ref, gg_ref, ug_ref, dg_ref,
           load_sem, store_sem, send_sem, recv_sem):
    gx, gy = lax.axis_index("gx"), lax.axis_index("gy")
    z, xh, c = gx // 4, (gx // 2) % 2, gx % 2
    y, xl = gy // 2, gy % 2

    def along(dz=0, other_x=False, other_core=False):
        zz = (z + dz + 16) % 16
        xx = 1 - xh if other_x else xh
        cc = 1 - c if other_core else c
        return (zz * 4 + xx * 2 + cc, gy)

    peers = [(dy, dx) for dy in (2, 1, 3, 0) for dx in (1, 0) if dy or dx]

    def across(dy, dx):
        return ((y + dy) % 4) * 2 + (xl + dx) % 2

    loads = [pltpu.make_async_copy(s, d, load_sem.at[i]) for i, (s, d) in enumerate((
        (tok_hbm, tok_ref), (grad_hbm, grad_ref), (gw_hbm, gw), (uw_hbm, uw), (dw_hbm, dw)))]
    for cp in loads:
        cp.start()

    barrier = pltpu.get_barrier_semaphore()
    met = [along(dz) for dz in (8, 4, -4, 2, -2, 1, -1)]
    met += [along(dz, other_x=True) for dz in (8, 4, -4, 0)]
    met += [along(other_core=True)]
    met += [(gx, across(dy, dx)) for dy, dx in peers]
    for dev in met:
        pl.semaphore_signal(barrier, inc=1, device_id=dev, device_id_type=MESH)

    loads[0].wait()
    loads[1].wait()
    first = c == 0
    tok, grad = tok_ref[...].astype(F32), grad_ref[...].astype(F32)
    mine = jnp.where(first, tok, grad)
    ex_out[...] = jnp.where(first, grad, tok)
    pl.semaphore_wait(barrier, len(met))

    sent = []

    def push(src, dst, dev):
        k = len(sent)
        cp = pltpu.make_async_remote_copy(
            src_ref=src, dst_ref=dst, send_sem=send_sem.at[k], recv_sem=recv_sem.at[k],
            device_id=dev, device_id_type=MESH)
        cp.start()
        sent.append(cp)
        return cp

    sibling = along(other_core=True)
    partner = along(other_x=True)

    push(ex_out, ex_in, sibling).wait_recv()
    theirs = ex_in[...]
    block = jnp.concatenate(
        [jnp.where(first, mine, theirs), jnp.where(first, theirs, mine)], axis=0)
    x[c, 0, 0, 0] = block.astype(BF16)

    shared, arriving = [], {}

    def share(n, f):
        ours = x.at[c, 0, n, f]
        from_x = push(ours, x.at[c, 1, n, f], partner)
        shared.append((push(ours, ours, sibling), from_x, n, f))

    def to_near(f):
        ours = x.at[c, 0, 0, f]
        if f < 2:
            arriving[3, f] = push(ours, x.at[c, 0, 3, f], along(-2))
        if f in (0, 3):
            arriving[3, (f + 3) % 4] = push(ours, x.at[c, 0, 3, (f + 3) % 4], along(2))
        for n in (1, 2):
            arriving[n, f] = push(ours, x.at[c, 0, n, f], along(-NEAR[n]))

    def pass_on(*slots):
        for slot in slots:
            arriving.pop(slot).wait_recv()
            share(*slot)

    for i in FAR_ORDER:
        arriving[0, 4 - i] = push(x.at[c, 0, 0, 0], x.at[c, 0, 0, 4 - i], along(4 * i))
    to_near(0)
    share(0, 0)
    pass_on((1, 0), (2, 0), (3, 0), (3, 3))
    for f in (1, 3, 2):
        arriving.pop((0, f)).wait_recv()
        to_near(f)
        share(0, f)
    pass_on((1, 1), (2, 1), (3, 1), (1, 3), (2, 3), (3, 2), (1, 2), (2, 2))

    def products(k):
        rows = x[0, k].reshape(256, 1024)
        for j, v in enumerate((
                dot(rows, gw[...], ((1,), (0,))), dot(rows, uw[...], ((1,), (0,))),
                dot(x[1, k].reshape(256, 1024), dw[...], ((1,), (1,))))):
            v = v.reshape(8, 32, 256)
            part[k, :, :, 256 * j:256 * j + 256] = v
            part_low[k, :, :, 256 * j:256 * j + 256] = v.astype(BF16)
        return [push(part_low.at[k, across(dy, dx)], b_in.at[k, s], (gx, across(dy, dx)))
                for s, (dy, dx) in enumerate(peers)]

    def pointwise(k, arrived):
        for cp in arrived:
            cp.wait_recv()
        total = part[k, gy]
        for s in range(7):
            total = total + b_in[k, s].astype(F32)
        gate, up, hgrad = total[:, 0:256], total[:, 256:512], total[:, 512:768]
        sigma = jax.nn.sigmoid(gate)
        act = gate * sigma
        h[k, gy, :, 0:256] = (hgrad * up * sigma * (1.0 + gate * (1.0 - sigma))).astype(BF16)
        h[k, gy, :, 256:512] = (hgrad * act).astype(BF16)
        hidden[k, gy] = (act * up).astype(BF16)
        return spread(k, h)

    def spread(k, ref):
        return [push(ref.at[k, gy], ref.at[k, gy], (gx, across(dy, dx))) for dy, dx in peers]

    def input_products(k, arrived):
        for cp in arrived:
            cp.wait_recv()
        hh = h[k].reshape(256, 512)
        for j in range(2):
            cols = slice(512 * j, 512 * j + 512)
            v = dot(hh[:, 0:256], gw[cols, :], ((1,), (1,)))
            v = v + dot(hh[:, 256:512], uw[cols, :], ((1,), (1,)))
            ig[k, :, :, :, :, cols] = v.reshape(4, 4, 2, 8, 512)
        return [push(ig.at[k, :, fs, 1 - c], core_in.at[k, :, fs], sibling)
                for fs in (pl.ds(2, 1), pl.ds(0, 2), pl.ds(3, 1))]

    def send_near(k, arrived):
        def terms(*fs):
            for n in range(4):
                for f in fs:
                    v = ig[k, n, f, c] + core_in[k, n, f]
                    v = jnp.concatenate([v[:, 0:512], v[:, 512:1024]], axis=0)
                    if n == 0:
                        near_own[k, f] = v
                    else:
                        near_out[k, n, f if n == 3 else PLACE[f]] = v.astype(BF16)

        def to(n, fs, dz):
            return push(near_out.at[k, n, fs], near_in.at[k, n, fs], along(dz))

        arrived[0].wait_recv()
        terms(2)
        early = [to(n, pl.ds(0, 1), NEAR[n]) for n in (1, 2)]
        for cp in arrived[1:]:
            cp.wait_recv()
        terms(0, 1, 3)
        late = [to(3, pl.ds(0, 2), 2), to(3, pl.ds(2, 2), -2)]
        return early, late + [to(n, pl.ds(1, 3), NEAR[n]) for n in (1, 2)]

    def send_far(k, early, late):
        out = []
        for cp in early:
            cp.wait_recv()
        for f in FAR_ORDER + (0,):
            if f == FAR_ORDER[1]:
                for cp in late:
                    cp.wait_recv()
            v = near_own[k, f]
            for n in (1, 2):
                v = v + near_in[k, n, PLACE[f]].astype(F32)
            if f < 2:
                v = v + near_in[k, 3, f].astype(F32)
            if f in (0, 3):
                v = v + near_in[k, 3, (f + 3) % 4].astype(F32)
            if k == 0 and f == 0:
                near_own[k, f] = v
            else:
                far_out[k, f] = v.astype(BF16)
                out.append(push(far_out.at[k, f], far_in.at[k, f],
                                along(4 * f, other_x=k == 1)))
        return out

    for cp in loads[2:]:
        cp.wait()
    for from_core, _, _, _ in shared:
        from_core.wait_recv()
    b0 = products(0)

    to_core = []
    for _, from_x, n, f in shared:
        from_x.wait_recv()
        other = x.at[c, 1, n, f]
        to_core.append(push(other, other, sibling))
    for cp in to_core:
        cp.wait_recv()
    b1 = products(1)

    c0 = pointwise(0, b0)
    c1 = pointwise(1, b1)
    i0 = input_products(0, c0)
    n0 = send_near(0, i0)
    spread_hidden = spread(0, hidden)
    i1 = input_products(1, c1)
    n1 = send_near(1, i1)
    spread_hidden += spread(1, hidden)
    f0 = send_far(0, *n0)
    f1 = send_far(1, *n1)

    for cp in spread_hidden:
        cp.wait_recv()
    factor = 1.0 / jnp.sqrt(F32(512))

    @pl.loop(0, 4)
    def _(i):
        cols = pl.ds(pl.multiple_of(i * 256, 256), 256)
        hh = h[...].reshape(512, 512)
        t = x[0, :, :, :, :, cols].reshape(512, 256)
        gg_ref[cols, :] = (dot(t, hh[:, 0:256], ((0,), (0,))) * factor).astype(BF16)
        ug_ref[cols, :] = (dot(t, hh[:, 256:512], ((0,), (0,))) * factor).astype(BF16)
        g = x[1, :, :, :, :, cols].reshape(512, 256)
        dg_ref[:, cols] = (dot(
            hidden[...].reshape(512, 256), g, ((0,), (0,))) * factor).astype(BF16)

    stores = [pltpu.make_async_copy(s, d, store_sem.at[i]) for i, (s, d) in enumerate((
        (gg_ref, gg_hbm), (ug_ref, ug_hbm), (dg_ref, dg_hbm), (ig_ref, ig_hbm)))]
    for cp in stores[:3]:
        cp.start()
    for cp in sent:
        cp.wait_send()
    for cp in f0 + f1:
        cp.wait_recv()
    v = near_own[0, 0] + far_in[1, 0].astype(F32)
    for f in (1, 2, 3):
        v = v + (far_in[0, f].astype(F32) + far_in[1, f].astype(F32))
    ig_ref[...] = jnp.concatenate([v[0:8], v[8:16]], axis=1).astype(BF16)

    stores[3].start()
    for cp in stores:
        cp.wait()


COPIES = 144


def place(*refs):
    given, wanted, held, load_sem, store_sem = refs[:4], refs[4:8], refs[8:12], refs[12], refs[13]
    loads = [pltpu.make_async_copy(s, v, load_sem.at[i])
             for i, (s, v) in enumerate(zip(given, held))]
    stores = [pltpu.make_async_copy(v, d, store_sem.at[i])
              for i, (v, d) in enumerate(zip(held, wanted))]
    for cp in loads:
        cp.start()
    for load, store in zip(loads, stores):
        load.wait()
        store.start()
    for cp in stores:
        cp.wait()


def per_device(tokens, out_grad, gate_weight, up_weight, down_weight):
    hbm = pl.BlockSpec(memory_space=pl.ANY)
    shape = jax.ShapeDtypeStruct
    outs = (shape((8, 1024), BF16), shape((1024, 256), BF16),
            shape((1024, 256), BF16), shape((256, 1024), BF16))
    results = pl.pallas_call(
        kernel,
        out_shape=outs,
        in_specs=[hbm] * 5,
        out_specs=(hbm,) * 4,
        scratch_shapes=[
            pltpu.VMEM((8, 1024), BF16),
            pltpu.VMEM((8, 1024), BF16),
            pltpu.VMEM((1024, 256), BF16),
            pltpu.VMEM((1024, 256), BF16),
            pltpu.VMEM((256, 1024), BF16),
            pltpu.VMEM((8, 1024), F32),
            pltpu.VMEM((8, 1024), F32),
            pltpu.VMEM((2, 2, 4, 4, 16, 1024), BF16),
            pltpu.VMEM((2, 8, 32, 768), F32),
            pltpu.VMEM((2, 8, 32, 768), BF16),
            pltpu.VMEM((2, 7, 32, 768), BF16),
            pltpu.VMEM((2, 8, 32, 512), BF16),
            pltpu.VMEM((2, 8, 32, 256), BF16),
            pltpu.VMEM((2, 4, 4, 2, 8, 1024), F32),
            pltpu.VMEM((2, 4, 4, 8, 1024), F32),
            pltpu.VMEM((2, 4, 4, 16, 512), BF16),
            pltpu.VMEM((2, 4, 16, 512), F32),
            pltpu.VMEM((2, 4, 4, 16, 512), BF16),
            pltpu.VMEM((2, 4, 16, 512), BF16),
            pltpu.VMEM((2, 4, 16, 512), BF16),
            pltpu.VMEM((8, 1024), BF16),
            pltpu.VMEM((1024, 256), BF16),
            pltpu.VMEM((1024, 256), BF16),
            pltpu.VMEM((256, 1024), BF16),
            pltpu.SemaphoreType.DMA((5,)),
            pltpu.SemaphoreType.DMA((4,)),
            pltpu.SemaphoreType.DMA((COPIES,)),
            pltpu.SemaphoreType.DMA((COPIES,)),
        ],
        compiler_params=pltpu.CompilerParams(
            collective_id=0, has_side_effects=True, vmem_limit_bytes=60 << 20),
        cost_estimate=pl.CostEstimate(
            flops=2 * 8 * 512 * 1024 * 256, bytes_accessed=4 << 20, transcendentals=64 * 256),
    )(tokens, out_grad, gate_weight, up_weight, down_weight)
    return pl.pallas_call(
        place,
        out_shape=outs,
        in_specs=[hbm] * 4,
        out_specs=(hbm,) * 4,
        scratch_shapes=[pltpu.VMEM(o.shape, BF16) for o in outs]
        + [pltpu.SemaphoreType.DMA((4,))] * 2,
        compiler_params=pltpu.CompilerParams(vmem_limit_bytes=60 << 20),
    )(*results)


def solution(mesh):
    return jax.shard_map(
        per_device,
        mesh=mesh,
        in_specs=(P("gx", "gy"), P("gx", "gy"), P("gy", "gx"), P("gy", "gx"), P("gx", "gy")),
        out_specs=(P("gx", "gy"), P("gy", "gx"), P("gy", "gx"), P("gx", "gy")),
        check_vma=False,
    )
```

```python
import jax
import jax.numpy as jnp
from jax import lax
from jax.experimental import pallas as pl
from jax.experimental.pallas import tpu as pltpu
from jax.sharding import PartitionSpec as P

MESH = pl.DeviceIdType.MESH
BF16, F32 = jnp.bfloat16, jnp.float32

NEAR = (0, 1, -1, 2)
FAR_ORDER = (2, 1, 3)
PLACE = (1, 2, 0, 3)


def dot(a, b, dims):
    return lax.dot_general(a, b, (dims, ((), ())), preferred_element_type=F32)


def kernel(tok_hbm, grad_hbm, gw_hbm, uw_hbm, dw_hbm,
           ig_hbm, gg_hbm, ug_hbm, dg_hbm,
           tok_ref, grad_ref, gw, uw, dw, ex_out, ex_in, x, part, part_low, b_in, h, hidden,
           ig, core_in,
           near_out, near_own, near_in, far_out, far_in,
           ig_ref, gg_ref, ug_ref, dg_ref,
           load_sem, store_sem, send_sem, recv_sem):
    gx, gy = lax.axis_index("gx"), lax.axis_index("gy")
    z, xh, c = gx // 4, (gx // 2) % 2, gx % 2
    y, xl = gy // 2, gy % 2

    def along(dz=0, other_x=False, other_core=False):
        zz = (z + dz + 16) % 16
        xx = 1 - xh if other_x else xh
        cc = 1 - c if other_core else c
        return (zz * 4 + xx * 2 + cc, gy)

    peers = [(dy, dx) for dy in (2, 1, 3, 0) for dx in (1, 0) if dy or dx]

    def across(dy, dx):
        return ((y + dy) % 4) * 2 + (xl + dx) % 2

    loads = [pltpu.make_async_copy(s, d, load_sem.at[i]) for i, (s, d) in enumerate((
        (tok_hbm, tok_ref), (grad_hbm, grad_ref), (gw_hbm, gw), (uw_hbm, uw), (dw_hbm, dw)))]
    for cp in loads:
        cp.start()

    barrier = pltpu.get_barrier_semaphore()
    met = [along(dz) for dz in (8, 4, -4, 2, -2, 1, -1)]
    met += [along(dz, other_x=True) for dz in (8, 4, -4, 1, -1, 0)]
    met += [along(other_core=True)]
    met += [(gx, across(dy, dx)) for dy, dx in peers]
    for dev in met:
        pl.semaphore_signal(barrier, inc=1, device_id=dev, device_id_type=MESH)

    loads[0].wait()
    loads[1].wait()
    first = c == 0
    tok, grad = tok_ref[...].astype(F32), grad_ref[...].astype(F32)
    mine = jnp.where(first, tok, grad)
    ex_out[...] = jnp.where(first, grad, tok)
    pl.semaphore_wait(barrier, len(met))

    sent = []

    def push(src, dst, dev):
        k = len(sent)
        cp = pltpu.make_async_remote_copy(
            src_ref=src, dst_ref=dst, send_sem=send_sem.at[k], recv_sem=recv_sem.at[k],
            device_id=dev, device_id_type=MESH)
        cp.start()
        sent.append(cp)
        return cp

    sibling = along(other_core=True)
    partner = along(other_x=True)

    push(ex_out, ex_in, sibling).wait_recv()
    theirs = ex_in[...]
    block = jnp.concatenate(
        [jnp.where(first, mine, theirs), jnp.where(first, theirs, mine)], axis=0)
    x[c, 0, 0, 0] = block.astype(BF16)

    shared, arriving, crossed = [], {}, {}

    def share(n, f):
        ours = x.at[c, 0, n, f]
        from_x = crossed.get((n, f)) or push(ours, x.at[c, 1, n, f], partner)
        shared.append((push(ours, ours, sibling), from_x, n, f))

    def to_near(f):
        ours = x.at[c, 0, 0, f]
        if f < 2:
            arriving[3, f] = push(ours, x.at[c, 0, 3, f], along(-2))
        if f in (0, 3):
            arriving[3, (f + 3) % 4] = push(ours, x.at[c, 0, 3, (f + 3) % 4], along(2))
        for n in (1, 2):
            arriving[n, f] = push(ours, x.at[c, 0, n, f], along(-NEAR[n]))
        if f == 2:
            for n in (1, 2):
                crossed[n, f] = push(ours, x.at[c, 1, n, f], along(-NEAR[n], other_x=True))

    def pass_on(*slots):
        for slot in slots:
            arriving.pop(slot).wait_recv()
            share(*slot)

    for i in FAR_ORDER:
        arriving[0, 4 - i] = push(x.at[c, 0, 0, 0], x.at[c, 0, 0, 4 - i], along(4 * i))
    to_near(0)
    share(0, 0)
    pass_on((1, 0), (2, 0), (3, 0), (3, 3))
    for f in (1, 3, 2):
        arriving.pop((0, f)).wait_recv()
        to_near(f)
        share(0, f)
    pass_on((1, 1), (2, 1), (3, 1), (1, 3), (2, 3), (3, 2), (1, 2), (2, 2))

    def products(k):
        rows = x[0, k].reshape(256, 1024)
        for j, v in enumerate((
                dot(rows, gw[...], ((1,), (0,))), dot(rows, uw[...], ((1,), (0,))),
                dot(x[1, k].reshape(256, 1024), dw[...], ((1,), (1,))))):
            v = v.reshape(8, 32, 256)
            part[k, :, :, 256 * j:256 * j + 256] = v
            part_low[k, :, :, 256 * j:256 * j + 256] = v.astype(BF16)
        return [push(part_low.at[k, across(dy, dx)], b_in.at[k, s], (gx, across(dy, dx)))
                for s, (dy, dx) in enumerate(peers)]

    def pointwise(k, arrived):
        for cp in arrived:
            cp.wait_recv()
        total = part[k, gy]
        for s in range(7):
            total = total + b_in[k, s].astype(F32)
        gate, up, hgrad = total[:, 0:256], total[:, 256:512], total[:, 512:768]
        sigma = jax.nn.sigmoid(gate)
        act = gate * sigma
        h[k, gy, :, 0:256] = (hgrad * up * sigma * (1.0 + gate * (1.0 - sigma))).astype(BF16)
        h[k, gy, :, 256:512] = (hgrad * act).astype(BF16)
        hidden[k, gy] = (act * up).astype(BF16)
        return spread(k, h)

    def spread(k, ref):
        return [push(ref.at[k, gy], ref.at[k, gy], (gx, across(dy, dx))) for dy, dx in peers]

    def input_products(k, arrived):
        for cp in arrived:
            cp.wait_recv()
        hh = h[k].reshape(256, 512)
        for j in range(2):
            cols = slice(512 * j, 512 * j + 512)
            v = dot(hh[:, 0:256], gw[cols, :], ((1,), (1,)))
            v = v + dot(hh[:, 256:512], uw[cols, :], ((1,), (1,)))
            ig[k, :, :, :, :, cols] = v.reshape(4, 4, 2, 8, 512)
        return [push(ig.at[k, :, fs, 1 - c], core_in.at[k, :, fs], sibling)
                for fs in (pl.ds(2, 1), pl.ds(0, 2), pl.ds(3, 1))]

    def send_near(k, arrived):
        def terms(*fs):
            for n in range(4):
                for f in fs:
                    v = ig[k, n, f, c] + core_in[k, n, f]
                    v = jnp.concatenate([v[:, 0:512], v[:, 512:1024]], axis=0)
                    if n == 0:
                        near_own[k, f] = v
                    else:
                        near_out[k, n, f if n == 3 else PLACE[f]] = v.astype(BF16)

        def to(n, fs, dz):
            return push(near_out.at[k, n, fs], near_in.at[k, n, fs], along(dz))

        arrived[0].wait_recv()
        terms(2)
        early = [to(n, pl.ds(0, 1), NEAR[n]) for n in (1, 2)]
        for cp in arrived[1:]:
            cp.wait_recv()
        terms(0, 1, 3)
        late = [to(3, pl.ds(0, 2), 2), to(3, pl.ds(2, 2), -2)]
        return early, late + [to(n, pl.ds(1, 3), NEAR[n]) for n in (1, 2)]

    def send_far(k, early, late):
        out = []
        for cp in early:
            cp.wait_recv()
        for f in FAR_ORDER + (0,):
            if f == FAR_ORDER[1]:
                for cp in late:
                    cp.wait_recv()
            v = near_own[k, f]
            for n in (1, 2):
                v = v + near_in[k, n, PLACE[f]].astype(F32)
            if f < 2:
                v = v + near_in[k, 3, f].astype(F32)
            if f in (0, 3):
                v = v + near_in[k, 3, (f + 3) % 4].astype(F32)
            if k == 0 and f == 0:
                near_own[k, f] = v
            else:
                far_out[k, f] = v.astype(BF16)
                out.append(push(far_out.at[k, f], far_in.at[k, f],
                                along(4 * f, other_x=k == 1)))
        return out

    for cp in loads[2:]:
        cp.wait()
    for from_core, _, _, _ in shared:
        from_core.wait_recv()
    b0 = products(0)

    to_core = []
    for _, from_x, n, f in shared:
        from_x.wait_recv()
        other = x.at[c, 1, n, f]
        to_core.append(push(other, other, sibling))
    for cp in to_core:
        cp.wait_recv()
    b1 = products(1)

    c0 = pointwise(0, b0)
    c1 = pointwise(1, b1)
    i0 = input_products(0, c0)
    n0 = send_near(0, i0)
    i1 = input_products(1, c1)
    n1 = send_near(1, i1)
    spread_hidden = spread(0, hidden) + spread(1, hidden)
    f0 = send_far(0, *n0)
    f1 = send_far(1, *n1)

    for cp in spread_hidden:
        cp.wait_recv()
    factor = 1.0 / jnp.sqrt(F32(512))

    @pl.loop(0, 4)
    def _(i):
        cols = pl.ds(pl.multiple_of(i * 256, 256), 256)
        hh = h[...].reshape(512, 512)
        t = x[0, :, :, :, :, cols].reshape(512, 256)
        gg_ref[cols, :] = (dot(t, hh[:, 0:256], ((0,), (0,))) * factor).astype(BF16)
        ug_ref[cols, :] = (dot(t, hh[:, 256:512], ((0,), (0,))) * factor).astype(BF16)
        g = x[1, :, :, :, :, cols].reshape(512, 256)
        dg_ref[:, cols] = (dot(
            hidden[...].reshape(512, 256), g, ((0,), (0,))) * factor).astype(BF16)

    stores = [pltpu.make_async_copy(s, d, store_sem.at[i]) for i, (s, d) in enumerate((
        (gg_ref, gg_hbm), (ug_ref, ug_hbm), (dg_ref, dg_hbm), (ig_ref, ig_hbm)))]
    for cp in stores[:3]:
        cp.start()
    for cp in sent:
        cp.wait_send()
    for cp in f0 + f1:
        cp.wait_recv()
    v = near_own[0, 0] + far_in[1, 0].astype(F32)
    for f in (1, 2, 3):
        v = v + (far_in[0, f].astype(F32) + far_in[1, f].astype(F32))
    ig_ref[...] = jnp.concatenate([v[0:8], v[8:16]], axis=1).astype(BF16)

    stores[3].start()
    for cp in stores:
        cp.wait()


COPIES = 144


def place(*refs):
    given, wanted, held, load_sem, store_sem = refs[:4], refs[4:8], refs[8:12], refs[12], refs[13]
    loads, stores = [], []
    for s, v, d in zip(given, held, wanted):
        parts = 1 if s.shape[0] == 8 else 4
        rows = s.shape[0] // parts
        for i in range(parts):
            cut = pl.ds(i * rows, rows)
            k = len(loads)
            loads.append(pltpu.make_async_copy(s.at[cut], v.at[cut], load_sem.at[k]))
            stores.append(pltpu.make_async_copy(v.at[cut], d.at[cut], store_sem.at[k]))
    for cp in loads:
        cp.start()
    for load, store in zip(loads, stores):
        load.wait()
        store.start()
    for cp in stores:
        cp.wait()


def per_device(tokens, out_grad, gate_weight, up_weight, down_weight):
    hbm = pl.BlockSpec(memory_space=pl.ANY)
    shape = jax.ShapeDtypeStruct
    outs = (shape((8, 1024), BF16), shape((1024, 256), BF16),
            shape((1024, 256), BF16), shape((256, 1024), BF16))
    results = pl.pallas_call(
        kernel,
        out_shape=outs,
        in_specs=[hbm] * 5,
        out_specs=(hbm,) * 4,
        scratch_shapes=[
            pltpu.VMEM((8, 1024), BF16),
            pltpu.VMEM((8, 1024), BF16),
            pltpu.VMEM((1024, 256), BF16),
            pltpu.VMEM((1024, 256), BF16),
            pltpu.VMEM((256, 1024), BF16),
            pltpu.VMEM((8, 1024), F32),
            pltpu.VMEM((8, 1024), F32),
            pltpu.VMEM((2, 2, 4, 4, 16, 1024), BF16),
            pltpu.VMEM((2, 8, 32, 768), F32),
            pltpu.VMEM((2, 8, 32, 768), BF16),
            pltpu.VMEM((2, 7, 32, 768), BF16),
            pltpu.VMEM((2, 8, 32, 512), BF16),
            pltpu.VMEM((2, 8, 32, 256), BF16),
            pltpu.VMEM((2, 4, 4, 2, 8, 1024), F32),
            pltpu.VMEM((2, 4, 4, 8, 1024), F32),
            pltpu.VMEM((2, 4, 4, 16, 512), BF16),
            pltpu.VMEM((2, 4, 16, 512), F32),
            pltpu.VMEM((2, 4, 4, 16, 512), BF16),
            pltpu.VMEM((2, 4, 16, 512), BF16),
            pltpu.VMEM((2, 4, 16, 512), BF16),
            pltpu.VMEM((8, 1024), BF16),
            pltpu.VMEM((1024, 256), BF16),
            pltpu.VMEM((1024, 256), BF16),
            pltpu.VMEM((256, 1024), BF16),
            pltpu.SemaphoreType.DMA((5,)),
            pltpu.SemaphoreType.DMA((4,)),
            pltpu.SemaphoreType.DMA((COPIES,)),
            pltpu.SemaphoreType.DMA((COPIES,)),
        ],
        compiler_params=pltpu.CompilerParams(
            collective_id=0, has_side_effects=True, vmem_limit_bytes=60 << 20),
        cost_estimate=pl.CostEstimate(
            flops=2 * 8 * 512 * 1024 * 256, bytes_accessed=4 << 20, transcendentals=64 * 256),
    )(tokens, out_grad, gate_weight, up_weight, down_weight)
    return pl.pallas_call(
        place,
        out_shape=outs,
        in_specs=[hbm] * 4,
        out_specs=(hbm,) * 4,
        scratch_shapes=[pltpu.VMEM(o.shape, BF16) for o in outs]
        + [pltpu.SemaphoreType.DMA((13,))] * 2,
        compiler_params=pltpu.CompilerParams(vmem_limit_bytes=60 << 20),
    )(*results)


def solution(mesh):
    return jax.shard_map(
        per_device,
        mesh=mesh,
        in_specs=(P("gx", "gy"), P("gx", "gy"), P("gy", "gx"), P("gy", "gx"), P("gx", "gy")),
        out_specs=(P("gx", "gy"), P("gy", "gx"), P("gy", "gx"), P("gx", "gy")),
        check_vma=False,
    )
```

```python
import jax
import jax.numpy as jnp
from jax import lax
from jax.experimental import pallas as pl
from jax.experimental.pallas import tpu as pltpu
from jax.sharding import PartitionSpec as P

MESH = pl.DeviceIdType.MESH
BF16, F32 = jnp.bfloat16, jnp.float32

NEAR = (0, 1, -1, 2)
FAR_ORDER = (2, 1, 3)
PLACE = (1, 2, 0, 3)


def dot(a, b, dims):
    return lax.dot_general(a, b, (dims, ((), ())), preferred_element_type=F32)


def kernel(tok_hbm, grad_hbm, gw_hbm, uw_hbm, dw_hbm,
           ig_hbm, gg_hbm, ug_hbm, dg_hbm,
           tok_ref, grad_ref, gw, uw, dw, ex_out, ex_in, x, part, part_low, b_in, h, hidden,
           ig, core_in,
           near_out, near_own, near_in, far_out, far_in,
           ig_ref, gg_ref, ug_ref, dg_ref,
           load_sem, store_sem, send_sem, recv_sem):
    gx, gy = lax.axis_index("gx"), lax.axis_index("gy")
    z, xh, c = gx // 4, (gx // 2) % 2, gx % 2
    y, xl = gy // 2, gy % 2

    def along(dz=0, other_x=False, other_core=False):
        zz = (z + dz + 16) % 16
        xx = 1 - xh if other_x else xh
        cc = 1 - c if other_core else c
        return (zz * 4 + xx * 2 + cc, gy)

    peers = [(dy, dx) for dy in (2, 1, 3, 0) for dx in (1, 0) if dy or dx]

    def across(dy, dx):
        return ((y + dy) % 4) * 2 + (xl + dx) % 2

    loads = [pltpu.make_async_copy(s, d, load_sem.at[i]) for i, (s, d) in enumerate((
        (tok_hbm, tok_ref), (grad_hbm, grad_ref), (gw_hbm, gw), (uw_hbm, uw), (dw_hbm, dw)))]
    for cp in loads:
        cp.start()

    barrier = pltpu.get_barrier_semaphore()
    met = [along(dz) for dz in (4, -4, 2, -2, 1, -1)]
    met += [along(dz, other_x=True) for dz in (4, -4, 1, -1, 0)]
    met += [along(other_core=True)]
    met += [(gx, across(dy, dx)) for dy, dx in peers]
    for dev in met:
        pl.semaphore_signal(barrier, inc=1, device_id=dev, device_id_type=MESH)

    loads[0].wait()
    loads[1].wait()
    first = c == 0
    tok, grad = tok_ref[...].astype(F32), grad_ref[...].astype(F32)
    mine = jnp.where(first, tok, grad)
    ex_out[...] = jnp.where(first, grad, tok)
    pl.semaphore_wait(barrier, len(met))

    sent = []

    def push(src, dst, dev):
        k = len(sent)
        cp = pltpu.make_async_remote_copy(
            src_ref=src, dst_ref=dst, send_sem=send_sem.at[k], recv_sem=recv_sem.at[k],
            device_id=dev, device_id_type=MESH)
        cp.start()
        sent.append(cp)
        return cp

    sibling = along(other_core=True)
    partner = along(other_x=True)

    push(ex_out, ex_in, sibling).wait_recv()
    theirs = ex_in[...]
    block = jnp.concatenate(
        [jnp.where(first, mine, theirs), jnp.where(first, theirs, mine)], axis=0)
    x[c, 0, 0, 0] = block.astype(BF16)

    shared, arriving, crossed = [], {}, {}

    def share(n, f):
        ours = x.at[c, 0, n, f]
        from_x = crossed.get((n, f)) or push(ours, x.at[c, 1, n, f], partner)
        shared.append((push(ours, ours, sibling), from_x, n, f))

    def to_near(f):
        ours = x.at[c, 0, 0, f]
        if f < 2:
            arriving[3, f] = push(ours, x.at[c, 0, 3, f], along(-2))
        if f in (0, 3):
            arriving[3, (f + 3) % 4] = push(ours, x.at[c, 0, 3, (f + 3) % 4], along(2))
        for n in (1, 2):
            arriving[n, f] = push(ours, x.at[c, 0, n, f], along(-NEAR[n]))
        if f == 2:
            for n in (1, 2):
                crossed[n, f] = push(ours, x.at[c, 1, n, f], along(-NEAR[n], other_x=True))

    def pass_on(*slots):
        for slot in slots:
            arriving.pop(slot).wait_recv()
            share(*slot)

    for i in (1, 3):
        arriving[0, 4 - i] = push(x.at[c, 0, 0, 0], x.at[c, 0, 0, 4 - i], along(4 * i))
    to_near(0)
    share(0, 0)
    pass_on((1, 0), (2, 0), (3, 0), (3, 3))
    halves = []
    for f, cols, dz in ((1, pl.ds(0, 512), -4), (3, pl.ds(512, 512), 4)):
        arriving.pop((0, f)).wait_recv()
        halves.append(push(x.at[c, 0, 0, f, :, cols], x.at[c, 0, 0, 2, :, cols], along(dz)))
        to_near(f)
        share(0, f)
    for cp in halves:
        cp.wait_recv()
    to_near(2)
    share(0, 2)
    pass_on((1, 1), (2, 1), (3, 1), (1, 3), (2, 3), (3, 2), (1, 2), (2, 2))

    def products(k):
        rows = x[0, k].reshape(256, 1024)
        for j, v in enumerate((
                dot(rows, gw[...], ((1,), (0,))), dot(rows, uw[...], ((1,), (0,))),
                dot(x[1, k].reshape(256, 1024), dw[...], ((1,), (1,))))):
            v = v.reshape(8, 32, 256)
            part[k, :, :, 256 * j:256 * j + 256] = v
            part_low[k, :, :, 256 * j:256 * j + 256] = v.astype(BF16)
        return [push(part_low.at[k, across(dy, dx)], b_in.at[k, s], (gx, across(dy, dx)))
                for s, (dy, dx) in enumerate(peers)]

    def pointwise(k, arrived):
        for cp in arrived:
            cp.wait_recv()
        total = part[k, gy]
        for s in range(7):
            total = total + b_in[k, s].astype(F32)
        gate, up, hgrad = total[:, 0:256], total[:, 256:512], total[:, 512:768]
        sigma = jax.nn.sigmoid(gate)
        act = gate * sigma
        h[k, gy, :, 0:256] = (hgrad * up * sigma * (1.0 + gate * (1.0 - sigma))).astype(BF16)
        h[k, gy, :, 256:512] = (hgrad * act).astype(BF16)
        hidden[k, gy] = (act * up).astype(BF16)
        return spread(k, h)

    def spread(k, ref):
        return [push(ref.at[k, gy], ref.at[k, gy], (gx, across(dy, dx))) for dy, dx in peers]

    def input_products(k, arrived):
        for cp in arrived:
            cp.wait_recv()
        hh = h[k].reshape(256, 512)
        for j in range(2):
            cols = slice(512 * j, 512 * j + 512)
            v = dot(hh[:, 0:256], gw[cols, :], ((1,), (1,)))
            v = v + dot(hh[:, 256:512], uw[cols, :], ((1,), (1,)))
            ig[k, :, :, :, :, cols] = v.reshape(4, 4, 2, 8, 512)
        return [push(ig.at[k, :, fs, 1 - c], core_in.at[k, :, fs], sibling)
                for fs in (pl.ds(2, 1), pl.ds(0, 2), pl.ds(3, 1))]

    def send_near(k, arrived):
        def terms(*fs):
            for n in range(4):
                for f in fs:
                    v = ig[k, n, f, c] + core_in[k, n, f]
                    v = jnp.concatenate([v[:, 0:512], v[:, 512:1024]], axis=0)
                    if n == 0:
                        near_own[k, f] = v
                    else:
                        near_out[k, n, f if n == 3 else PLACE[f]] = v.astype(BF16)

        def to(n, fs, dz):
            return push(near_out.at[k, n, fs], near_in.at[k, n, fs], along(dz))

        arrived[0].wait_recv()
        terms(2)
        early = [to(n, pl.ds(0, 1), NEAR[n]) for n in (1, 2)]
        for cp in arrived[1:]:
            cp.wait_recv()
        terms(0, 1, 3)
        late = [to(3, pl.ds(0, 2), 2), to(3, pl.ds(2, 2), -2)]
        return early, late + [to(n, pl.ds(1, 3), NEAR[n]) for n in (1, 2)]

    def send_far(k, early, late):
        out = []
        for cp in early:
            cp.wait_recv()
        for f in FAR_ORDER + (0,):
            if f == FAR_ORDER[1]:
                for cp in late:
                    cp.wait_recv()
            v = near_own[k, f]
            for n in (1, 2):
                v = v + near_in[k, n, PLACE[f]].astype(F32)
            if f < 2:
                v = v + near_in[k, 3, f].astype(F32)
            if f in (0, 3):
                v = v + near_in[k, 3, (f + 3) % 4].astype(F32)
            if k == 0 and f == 0:
                near_own[k, f] = v
            else:
                far_out[k, f] = v.astype(BF16)
                out.append(push(far_out.at[k, f], far_in.at[k, f],
                                along(4 * f, other_x=k == 1)))
        return out

    for cp in loads[2:]:
        cp.wait()
    for from_core, _, _, _ in shared:
        from_core.wait_recv()
    b0 = products(0)

    to_core = []
    for _, from_x, n, f in shared:
        from_x.wait_recv()
        other = x.at[c, 1, n, f]
        to_core.append(push(other, other, sibling))
    for cp in to_core:
        cp.wait_recv()
    b1 = products(1)

    c0 = pointwise(0, b0)
    c1 = pointwise(1, b1)
    i0 = input_products(0, c0)
    n0 = send_near(0, i0)
    i1 = input_products(1, c1)
    n1 = send_near(1, i1)
    spread_hidden = spread(0, hidden) + spread(1, hidden)
    f0 = send_far(0, *n0)
    f1 = send_far(1, *n1)

    for cp in spread_hidden:
        cp.wait_recv()
    factor = 1.0 / jnp.sqrt(F32(512))

    @pl.loop(0, 4)
    def _(i):
        cols = pl.ds(pl.multiple_of(i * 256, 256), 256)
        hh = h[...].reshape(512, 512)
        t = x[0, :, :, :, :, cols].reshape(512, 256)
        gg_ref[cols, :] = (dot(t, hh[:, 0:256], ((0,), (0,))) * factor).astype(BF16)
        ug_ref[cols, :] = (dot(t, hh[:, 256:512], ((0,), (0,))) * factor).astype(BF16)
        g = x[1, :, :, :, :, cols].reshape(512, 256)
        dg_ref[:, cols] = (dot(
            hidden[...].reshape(512, 256), g, ((0,), (0,))) * factor).astype(BF16)

    stores = [pltpu.make_async_copy(s, d, store_sem.at[i]) for i, (s, d) in enumerate((
        (gg_ref, gg_hbm), (ug_ref, ug_hbm), (dg_ref, dg_hbm), (ig_ref, ig_hbm)))]
    for cp in stores[:3]:
        cp.start()
    for cp in sent:
        cp.wait_send()
    for cp in f0 + f1:
        cp.wait_recv()
    v = near_own[0, 0] + far_in[1, 0].astype(F32)
    for f in (1, 2, 3):
        v = v + (far_in[0, f].astype(F32) + far_in[1, f].astype(F32))
    ig_ref[...] = jnp.concatenate([v[0:8], v[8:16]], axis=1).astype(BF16)

    stores[3].start()
    for cp in stores:
        cp.wait()


COPIES = 144


def place(*refs):
    given, wanted, held, load_sem, store_sem = refs[:4], refs[4:8], refs[8:12], refs[12], refs[13]
    loads, stores = [], []
    for s, v, d in zip(given, held, wanted):
        parts = 1 if s.shape[0] == 8 else 4
        rows = s.shape[0] // parts
        for i in range(parts):
            cut = pl.ds(i * rows, rows)
            k = len(loads)
            loads.append(pltpu.make_async_copy(s.at[cut], v.at[cut], load_sem.at[k]))
            stores.append(pltpu.make_async_copy(v.at[cut], d.at[cut], store_sem.at[k]))
    for cp in loads:
        cp.start()
    for load, store in zip(loads, stores):
        load.wait()
        store.start()
    for cp in stores:
        cp.wait()


def per_device(tokens, out_grad, gate_weight, up_weight, down_weight):
    hbm = pl.BlockSpec(memory_space=pl.ANY)
    shape = jax.ShapeDtypeStruct
    outs = (shape((8, 1024), BF16), shape((1024, 256), BF16),
            shape((1024, 256), BF16), shape((256, 1024), BF16))
    results = pl.pallas_call(
        kernel,
        out_shape=outs,
        in_specs=[hbm] * 5,
        out_specs=(hbm,) * 4,
        scratch_shapes=[
            pltpu.VMEM((8, 1024), BF16),
            pltpu.VMEM((8, 1024), BF16),
            pltpu.VMEM((1024, 256), BF16),
            pltpu.VMEM((1024, 256), BF16),
            pltpu.VMEM((256, 1024), BF16),
            pltpu.VMEM((8, 1024), F32),
            pltpu.VMEM((8, 1024), F32),
            pltpu.VMEM((2, 2, 4, 4, 16, 1024), BF16),
            pltpu.VMEM((2, 8, 32, 768), F32),
            pltpu.VMEM((2, 8, 32, 768), BF16),
            pltpu.VMEM((2, 7, 32, 768), BF16),
            pltpu.VMEM((2, 8, 32, 512), BF16),
            pltpu.VMEM((2, 8, 32, 256), BF16),
            pltpu.VMEM((2, 4, 4, 2, 8, 1024), F32),
            pltpu.VMEM((2, 4, 4, 8, 1024), F32),
            pltpu.VMEM((2, 4, 4, 16, 512), BF16),
            pltpu.VMEM((2, 4, 16, 512), F32),
            pltpu.VMEM((2, 4, 4, 16, 512), BF16),
            pltpu.VMEM((2, 4, 16, 512), BF16),
            pltpu.VMEM((2, 4, 16, 512), BF16),
            pltpu.VMEM((8, 1024), BF16),
            pltpu.VMEM((1024, 256), BF16),
            pltpu.VMEM((1024, 256), BF16),
            pltpu.VMEM((256, 1024), BF16),
            pltpu.SemaphoreType.DMA((5,)),
            pltpu.SemaphoreType.DMA((4,)),
            pltpu.SemaphoreType.DMA((COPIES,)),
            pltpu.SemaphoreType.DMA((COPIES,)),
        ],
        compiler_params=pltpu.CompilerParams(
            collective_id=0, has_side_effects=True, vmem_limit_bytes=60 << 20),
        cost_estimate=pl.CostEstimate(
            flops=2 * 8 * 512 * 1024 * 256, bytes_accessed=4 << 20, transcendentals=64 * 256),
    )(tokens, out_grad, gate_weight, up_weight, down_weight)
    return pl.pallas_call(
        place,
        out_shape=outs,
        in_specs=[hbm] * 4,
        out_specs=(hbm,) * 4,
        scratch_shapes=[pltpu.VMEM(o.shape, BF16) for o in outs]
        + [pltpu.SemaphoreType.DMA((13,))] * 2,
        compiler_params=pltpu.CompilerParams(vmem_limit_bytes=60 << 20),
    )(*results)


def solution(mesh):
    return jax.shard_map(
        per_device,
        mesh=mesh,
        in_specs=(P("gx", "gy"), P("gx", "gy"), P("gy", "gx"), P("gy", "gx"), P("gx", "gy")),
        out_specs=(P("gx", "gy"), P("gy", "gx"), P("gy", "gx"), P("gx", "gy")),
        check_vma=False,
    )
```

```python
import jax
import jax.numpy as jnp
from jax import lax
from jax.experimental import pallas as pl
from jax.experimental.pallas import tpu as pltpu
from jax.sharding import PartitionSpec as P

MESH = pl.DeviceIdType.MESH
BF16, F32 = jnp.bfloat16, jnp.float32

NEAR = (0, 1, -1, 2)
FAR_ORDER = (2, 1, 3)
PLACE = (1, 2, 0, 3)


def dot(a, b, dims):
    return lax.dot_general(a, b, (dims, ((), ())), preferred_element_type=F32)


def kernel(tok_hbm, grad_hbm, gw_hbm, uw_hbm, dw_hbm,
           ig_hbm, gg_hbm, ug_hbm, dg_hbm,
           tok_ref, grad_ref, gw, uw, dw, ex_out, ex_in, x, part, part_low, b_in, h, hidden,
           ig, core_in,
           near_out, near_own, near_in, far_out, far_in,
           ig_ref, gg_ref, ug_ref, dg_ref,
           load_sem, store_sem, send_sem, recv_sem):
    gx, gy = lax.axis_index("gx"), lax.axis_index("gy")
    z, xh, c = gx // 4, (gx // 2) % 2, gx % 2
    y, xl = gy // 2, gy % 2

    def along(dz=0, other_x=False, other_core=False):
        zz = (z + dz + 16) % 16
        xx = 1 - xh if other_x else xh
        cc = 1 - c if other_core else c
        return (zz * 4 + xx * 2 + cc, gy)

    peers = [(dy, dx) for dy in (2, 1, 3, 0) for dx in (1, 0) if dy or dx]

    def across(dy, dx):
        return ((y + dy) % 4) * 2 + (xl + dx) % 2

    loads = [pltpu.make_async_copy(s, d, load_sem.at[i]) for i, (s, d) in enumerate((
        (tok_hbm, tok_ref), (grad_hbm, grad_ref), (gw_hbm, gw), (uw_hbm, uw), (dw_hbm, dw)))]
    for cp in loads:
        cp.start()

    barrier = pltpu.get_barrier_semaphore()
    met = [along(dz) for dz in (4, -4, 2, -2, 1, -1)]
    met += [along(dz, other_x=True) for dz in (1, -1, 0)]
    met += [along(other_core=True)]
    met += [(gx, across(dy, dx)) for dy, dx in peers]
    for dev in met:
        pl.semaphore_signal(barrier, inc=1, device_id=dev, device_id_type=MESH)

    loads[0].wait()
    loads[1].wait()
    first = c == 0
    tok, grad = tok_ref[...].astype(F32), grad_ref[...].astype(F32)
    mine = jnp.where(first, tok, grad)
    ex_out[...] = jnp.where(first, grad, tok)
    pl.semaphore_wait(barrier, len(met))

    sent = []

    def push(src, dst, dev):
        k = len(sent)
        cp = pltpu.make_async_remote_copy(
            src_ref=src, dst_ref=dst, send_sem=send_sem.at[k], recv_sem=recv_sem.at[k],
            device_id=dev, device_id_type=MESH)
        cp.start()
        sent.append(cp)
        return cp

    sibling = along(other_core=True)
    partner = along(other_x=True)

    push(ex_out, ex_in, sibling).wait_recv()
    theirs = ex_in[...]
    block = jnp.concatenate(
        [jnp.where(first, mine, theirs), jnp.where(first, theirs, mine)], axis=0)
    x[c, 0, 0, 0] = block.astype(BF16)

    shared, arriving, crossed = [], {}, {}

    def share(n, f):
        ours = x.at[c, 0, n, f]
        from_x = crossed.get((n, f)) or push(ours, x.at[c, 1, n, f], partner)
        shared.append((push(ours, ours, sibling), from_x, n, f))

    def to_near(f):
        ours = x.at[c, 0, 0, f]
        if f < 2:
            arriving[3, f] = push(ours, x.at[c, 0, 3, f], along(-2))
        if f in (0, 3):
            arriving[3, (f + 3) % 4] = push(ours, x.at[c, 0, 3, (f + 3) % 4], along(2))
        for n in (1, 2):
            arriving[n, f] = push(ours, x.at[c, 0, n, f], along(-NEAR[n]))
        if f == 2:
            for n in (1, 2):
                crossed[n, f] = push(ours, x.at[c, 1, n, f], along(-NEAR[n], other_x=True))

    def pass_on(*slots):
        for slot in slots:
            arriving.pop(slot).wait_recv()
            share(*slot)

    for i in (1, 3):
        arriving[0, 4 - i] = push(x.at[c, 0, 0, 0], x.at[c, 0, 0, 4 - i], along(4 * i))
    to_near(0)
    share(0, 0)
    pass_on((1, 0), (2, 0), (3, 0), (3, 3))
    halves = []
    for f, cols, dz in ((1, pl.ds(0, 512), -4), (3, pl.ds(512, 512), 4)):
        arriving.pop((0, f)).wait_recv()
        halves.append(push(x.at[c, 0, 0, f, :, cols], x.at[c, 0, 0, 2, :, cols], along(dz)))
        to_near(f)
        share(0, f)
    for cp in halves:
        cp.wait_recv()
    to_near(2)
    share(0, 2)
    pass_on((1, 1), (2, 1), (3, 1), (1, 3), (2, 3), (3, 2), (1, 2), (2, 2))

    def products(k):
        rows = x[0, k].reshape(256, 1024)
        for j, v in enumerate((
                dot(rows, gw[...], ((1,), (0,))), dot(rows, uw[...], ((1,), (0,))),
                dot(x[1, k].reshape(256, 1024), dw[...], ((1,), (1,))))):
            v = v.reshape(8, 32, 256)
            part[k, :, :, 256 * j:256 * j + 256] = v
            part_low[k, :, :, 256 * j:256 * j + 256] = v.astype(BF16)
        return [push(part_low.at[k, across(dy, dx)], b_in.at[k, s], (gx, across(dy, dx)))
                for s, (dy, dx) in enumerate(peers)]

    def pointwise(k, arrived):
        for cp in arrived:
            cp.wait_recv()
        total = part[k, gy]
        for s in range(7):
            total = total + b_in[k, s].astype(F32)
        gate, up, hgrad = total[:, 0:256], total[:, 256:512], total[:, 512:768]
        sigma = jax.nn.sigmoid(gate)
        act = gate * sigma
        h[k, gy, :, 0:256] = (hgrad * up * sigma * (1.0 + gate * (1.0 - sigma))).astype(BF16)
        h[k, gy, :, 256:512] = (hgrad * act).astype(BF16)
        hidden[k, gy] = (act * up).astype(BF16)
        return spread(k, h)

    def spread(k, ref):
        return [push(ref.at[k, gy], ref.at[k, gy], (gx, across(dy, dx))) for dy, dx in peers]

    def input_products(k, arrived):
        for cp in arrived:
            cp.wait_recv()
        hh = h[k].reshape(256, 512)
        for j in range(2):
            cols = slice(512 * j, 512 * j + 512)
            v = dot(hh[:, 0:256], gw[cols, :], ((1,), (1,)))
            v = v + dot(hh[:, 256:512], uw[cols, :], ((1,), (1,)))
            ig[k, :, :, :, :, cols] = v.reshape(4, 4, 2, 8, 512)
        return [push(ig.at[k, :, fs, 1 - c], core_in.at[k, :, fs], sibling)
                for fs in (pl.ds(2, 1), pl.ds(0, 2), pl.ds(3, 1))]

    def send_near(k, arrived):
        def terms(*fs):
            for n in range(4):
                for f in fs:
                    v = ig[k, n, f, c] + core_in[k, n, f]
                    v = jnp.concatenate([v[:, 0:512], v[:, 512:1024]], axis=0)
                    if n == 0:
                        near_own[k, f] = v
                    else:
                        near_out[k, n, f if n == 3 else PLACE[f]] = v.astype(BF16)

        def to(n, fs, dz):
            return push(near_out.at[k, n, fs], near_in.at[k, n, fs], along(dz))

        arrived[0].wait_recv()
        terms(2)
        early = [to(n, pl.ds(0, 1), NEAR[n]) for n in (1, 2)]
        for cp in arrived[1:]:
            cp.wait_recv()
        terms(0, 1, 3)
        late = [to(3, pl.ds(0, 2), 2), to(3, pl.ds(2, 2), -2)]
        return early, late + [to(n, pl.ds(1, 3), NEAR[n]) for n in (1, 2)]

    def send_far(k, early, late):
        out = []
        for cp in early:
            cp.wait_recv()
        for f in FAR_ORDER + (0,):
            if f == FAR_ORDER[1]:
                for cp in late:
                    cp.wait_recv()
            v = near_own[k, f]
            for n in (1, 2):
                v = v + near_in[k, n, PLACE[f]].astype(F32)
            if f < 2:
                v = v + near_in[k, 3, f].astype(F32)
            if f in (0, 3):
                v = v + near_in[k, 3, (f + 3) % 4].astype(F32)
            if k == 0 and f == 0:
                near_own[k, f] = v
            else:
                far_out[k, f] = v.astype(BF16)
                out.append(push(far_out.at[k, f], far_in.at[k, f],
                                along(4 * f, other_x=k == 1)))
        return out

    for cp in loads[2:]:
        cp.wait()
    for from_core, _, _, _ in shared:
        from_core.wait_recv()
    b0 = products(0)

    to_core = []
    for _, from_x, n, f in shared:
        from_x.wait_recv()
        other = x.at[c, 1, n, f]
        to_core.append(push(other, other, sibling))
    for cp in to_core:
        cp.wait_recv()
    b1 = products(1)

    c0 = pointwise(0, b0)
    c1 = pointwise(1, b1)
    i0 = input_products(0, c0)
    n0 = send_near(0, i0)
    i1 = input_products(1, c1)
    n1 = send_near(1, i1)
    spread_hidden = spread(0, hidden) + spread(1, hidden)
    f0 = send_far(0, *n0)
    f1 = send_far(1, *n1)

    for cp in spread_hidden:
        cp.wait_recv()
    factor = 1.0 / jnp.sqrt(F32(512))

    @pl.loop(0, 4)
    def _(i):
        cols = pl.ds(pl.multiple_of(i * 256, 256), 256)
        hh = h[...].reshape(512, 512)
        t = x[0, :, :, :, :, cols].reshape(512, 256)
        gg_ref[cols, :] = (dot(t, hh[:, 0:256], ((0,), (0,))) * factor).astype(BF16)
        ug_ref[cols, :] = (dot(t, hh[:, 256:512], ((0,), (0,))) * factor).astype(BF16)
        g = x[1, :, :, :, :, cols].reshape(512, 256)
        dg_ref[:, cols] = (dot(
            hidden[...].reshape(512, 256), g, ((0,), (0,))) * factor).astype(BF16)

    stores = [pltpu.make_async_copy(s, d, store_sem.at[i]) for i, (s, d) in enumerate((
        (gg_ref, gg_hbm), (ug_ref, ug_hbm), (dg_ref, dg_hbm), (ig_ref, ig_hbm)))]
    for cp in stores[:3]:
        cp.start()
    for cp in sent:
        cp.wait_send()
    for cp in f0 + f1:
        cp.wait_recv()
    v = near_own[0, 0] + far_in[1, 0].astype(F32)
    for f in (1, 2, 3):
        v = v + (far_in[0, f].astype(F32) + far_in[1, f].astype(F32))
    ig_ref[...] = jnp.concatenate([v[0:8], v[8:16]], axis=1).astype(BF16)

    stores[3].start()
    for cp in stores:
        cp.wait()


COPIES = 144


def place(*refs):
    given, wanted, held, load_sem, store_sem = refs[:4], refs[4:8], refs[8:12], refs[12], refs[13]
    loads, stores = [], []
    for s, v, d in zip(given, held, wanted):
        parts = 1 if s.shape[0] == 8 else 4
        rows = s.shape[0] // parts
        for i in range(parts):
            cut = pl.ds(i * rows, rows)
            k = len(loads)
            loads.append(pltpu.make_async_copy(s.at[cut], v.at[cut], load_sem.at[k]))
            stores.append(pltpu.make_async_copy(v.at[cut], d.at[cut], store_sem.at[k]))
    for cp in loads:
        cp.start()
    for load, store in zip(loads, stores):
        load.wait()
        store.start()
    for cp in stores:
        cp.wait()


def per_device(tokens, out_grad, gate_weight, up_weight, down_weight):
    hbm = pl.BlockSpec(memory_space=pl.ANY)
    shape = jax.ShapeDtypeStruct
    outs = (shape((8, 1024), BF16), shape((1024, 256), BF16),
            shape((1024, 256), BF16), shape((256, 1024), BF16))
    results = pl.pallas_call(
        kernel,
        out_shape=outs,
        in_specs=[hbm] * 5,
        out_specs=(hbm,) * 4,
        scratch_shapes=[
            pltpu.VMEM((8, 1024), BF16),
            pltpu.VMEM((8, 1024), BF16),
            pltpu.VMEM((1024, 256), BF16),
            pltpu.VMEM((1024, 256), BF16),
            pltpu.VMEM((256, 1024), BF16),
            pltpu.VMEM((8, 1024), F32),
            pltpu.VMEM((8, 1024), F32),
            pltpu.VMEM((2, 2, 4, 4, 16, 1024), BF16),
            pltpu.VMEM((2, 8, 32, 768), F32),
            pltpu.VMEM((2, 8, 32, 768), BF16),
            pltpu.VMEM((2, 7, 32, 768), BF16),
            pltpu.VMEM((2, 8, 32, 512), BF16),
            pltpu.VMEM((2, 8, 32, 256), BF16),
            pltpu.VMEM((2, 4, 4, 2, 8, 1024), F32),
            pltpu.VMEM((2, 4, 4, 8, 1024), F32),
            pltpu.VMEM((2, 4, 4, 16, 512), BF16),
            pltpu.VMEM((2, 4, 16, 512), F32),
            pltpu.VMEM((2, 4, 4, 16, 512), BF16),
            pltpu.VMEM((2, 4, 16, 512), BF16),
            pltpu.VMEM((2, 4, 16, 512), BF16),
            pltpu.VMEM((8, 1024), BF16),
            pltpu.VMEM((1024, 256), BF16),
            pltpu.VMEM((1024, 256), BF16),
            pltpu.VMEM((256, 1024), BF16),
            pltpu.SemaphoreType.DMA((5,)),
            pltpu.SemaphoreType.DMA((4,)),
            pltpu.SemaphoreType.DMA((COPIES,)),
            pltpu.SemaphoreType.DMA((COPIES,)),
        ],
        compiler_params=pltpu.CompilerParams(
            collective_id=0, has_side_effects=True, vmem_limit_bytes=60 << 20),
        cost_estimate=pl.CostEstimate(
            flops=2 * 8 * 512 * 1024 * 256, bytes_accessed=4 << 20, transcendentals=64 * 256),
    )(tokens, out_grad, gate_weight, up_weight, down_weight)
    return pl.pallas_call(
        place,
        out_shape=outs,
        in_specs=[hbm] * 4,
        out_specs=(hbm,) * 4,
        scratch_shapes=[pltpu.VMEM(o.shape, BF16) for o in outs]
        + [pltpu.SemaphoreType.DMA((13,))] * 2,
        compiler_params=pltpu.CompilerParams(vmem_limit_bytes=60 << 20),
    )(*results)


def solution(mesh):
    return jax.shard_map(
        per_device,
        mesh=mesh,
        in_specs=(P("gx", "gy"), P("gx", "gy"), P("gy", "gx"), P("gy", "gx"), P("gx", "gy")),
        out_specs=(P("gx", "gy"), P("gy", "gx"), P("gy", "gx"), P("gx", "gy")),
        check_vma=False,
    )
```

```python
import jax
import jax.numpy as jnp
from jax import lax
from jax.experimental import pallas as pl
from jax.experimental.pallas import tpu as pltpu
from jax.sharding import PartitionSpec as P

MESH = pl.DeviceIdType.MESH
BF16, F32 = jnp.bfloat16, jnp.float32

NEAR = (0, 1, -1, 2)
FAR_ORDER = (2, 1, 3)
PLACE = (1, 2, 0, 3)


def dot(a, b, dims):
    return lax.dot_general(a, b, (dims, ((), ())), preferred_element_type=F32)


def kernel(tok_hbm, grad_hbm, gw_hbm, uw_hbm, dw_hbm,
           ig_hbm, gg_hbm, ug_hbm, dg_hbm,
           tok_ref, grad_ref, gw, uw, dw, ex_out, ex_in, x, part, part_low, b_in, h, hidden,
           ig, core_in,
           near_out, near_own, near_in, far_out, far_in,
           ig_ref, gg_ref, ug_ref, dg_ref,
           load_sem, store_sem, send_sem, recv_sem):
    gx, gy = lax.axis_index("gx"), lax.axis_index("gy")
    z, xh, c = gx // 4, (gx // 2) % 2, gx % 2
    y, xl = gy // 2, gy % 2

    def along(dz=0, other_x=False, other_core=False):
        zz = (z + dz + 16) % 16
        xx = 1 - xh if other_x else xh
        cc = 1 - c if other_core else c
        return (zz * 4 + xx * 2 + cc, gy)

    peers = [(dy, dx) for dy in (2, 1, 3, 0) for dx in (1, 0) if dy or dx]

    def across(dy, dx):
        return ((y + dy) % 4) * 2 + (xl + dx) % 2

    loads = [pltpu.make_async_copy(s, d, load_sem.at[i]) for i, (s, d) in enumerate((
        (tok_hbm, tok_ref), (grad_hbm, grad_ref), (gw_hbm, gw), (uw_hbm, uw), (dw_hbm, dw)))]
    for cp in loads:
        cp.start()

    barrier = pltpu.get_barrier_semaphore()
    met = [along(dz) for dz in (4, -4, 2, -2, 1, -1)]
    met += [along(dz, other_x=True) for dz in (1, -1, 0)]
    met += [along(other_core=True)]
    met += [(gx, across(dy, dx)) for dy, dx in peers]
    for dev in met:
        pl.semaphore_signal(barrier, inc=1, device_id=dev, device_id_type=MESH)

    loads[0].wait()
    loads[1].wait()
    first = c == 0
    tok, grad = tok_ref[...].astype(F32), grad_ref[...].astype(F32)
    mine = jnp.where(first, tok, grad)
    ex_out[...] = jnp.where(first, grad, tok)
    pl.semaphore_wait(barrier, len(met))

    sent = []

    def push(src, dst, dev):
        k = len(sent)
        cp = pltpu.make_async_remote_copy(
            src_ref=src, dst_ref=dst, send_sem=send_sem.at[k], recv_sem=recv_sem.at[k],
            device_id=dev, device_id_type=MESH)
        cp.start()
        sent.append(cp)
        return cp

    sibling = along(other_core=True)
    partner = along(other_x=True)

    push(ex_out, ex_in, sibling).wait_recv()
    theirs = ex_in[...]
    block = jnp.concatenate(
        [jnp.where(first, mine, theirs), jnp.where(first, theirs, mine)], axis=0)
    x[c, 0, 0, 0] = block.astype(BF16)

    shared, arriving, crossed = [], {}, {}

    def share(n, f):
        ours = x.at[c, 0, n, f]
        from_x = crossed.get((n, f)) or push(ours, x.at[c, 1, n, f], partner)
        shared.append((push(ours, ours, sibling), from_x, n, f))

    def to_near(f):
        ours = x.at[c, 0, 0, f]
        if f < 2:
            arriving[3, f] = push(ours, x.at[c, 0, 3, f], along(-2))
        if f in (0, 3):
            arriving[3, (f + 3) % 4] = push(ours, x.at[c, 0, 3, (f + 3) % 4], along(2))
        for n in (1, 2):
            arriving[n, f] = push(ours, x.at[c, 0, n, f], along(-NEAR[n]))
        if f == 2:
            for n in (1, 2):
                crossed[n, f] = push(ours, x.at[c, 1, n, f], along(-NEAR[n], other_x=True))

    def pass_on(*slots):
        for slot in slots:
            arriving.pop(slot).wait_recv()
            share(*slot)

    for i in (1, 3):
        arriving[0, 4 - i] = push(x.at[c, 0, 0, 0], x.at[c, 0, 0, 4 - i], along(4 * i))
    to_near(0)
    share(0, 0)
    pass_on((1, 0), (2, 0), (3, 0), (3, 3))
    halves = []
    for f, cols, dz in ((1, pl.ds(0, 512), -4), (3, pl.ds(512, 512), 4)):
        arriving.pop((0, f)).wait_recv()
        halves.append(push(x.at[c, 0, 0, f, :, cols], x.at[c, 0, 0, 2, :, cols], along(dz)))
    for f in (1, 3):
        to_near(f)
        share(0, f)
    for cp in halves:
        cp.wait_recv()
    to_near(2)
    share(0, 2)
    pass_on((1, 1), (2, 1), (3, 1), (1, 3), (2, 3), (3, 2), (1, 2), (2, 2))

    def products(k):
        rows = x[0, k].reshape(256, 1024)
        for j, v in enumerate((
                dot(rows, gw[...], ((1,), (0,))), dot(rows, uw[...], ((1,), (0,))),
                dot(x[1, k].reshape(256, 1024), dw[...], ((1,), (1,))))):
            v = v.reshape(8, 32, 256)
            part[k, :, :, 256 * j:256 * j + 256] = v
            part_low[k, :, :, 256 * j:256 * j + 256] = v.astype(BF16)
        return [push(part_low.at[k, across(dy, dx)], b_in.at[k, s], (gx, across(dy, dx)))
                for s, (dy, dx) in enumerate(peers)]

    def pointwise(k, arrived):
        for cp in arrived:
            cp.wait_recv()
        total = part[k, gy]
        for s in range(7):
            total = total + b_in[k, s].astype(F32)
        gate, up, hgrad = total[:, 0:256], total[:, 256:512], total[:, 512:768]
        sigma = jax.nn.sigmoid(gate)
        act = gate * sigma
        h[k, gy, :, 0:256] = (hgrad * up * sigma * (1.0 + gate * (1.0 - sigma))).astype(BF16)
        h[k, gy, :, 256:512] = (hgrad * act).astype(BF16)
        hidden[k, gy] = (act * up).astype(BF16)
        return spread(k, h)

    def spread(k, ref):
        return [push(ref.at[k, gy], ref.at[k, gy], (gx, across(dy, dx))) for dy, dx in peers]

    def input_products(k, arrived):
        for cp in arrived:
            cp.wait_recv()
        hh = h[k].reshape(256, 512)
        for j in range(2):
            cols = slice(512 * j, 512 * j + 512)
            v = dot(hh[:, 0:256], gw[cols, :], ((1,), (1,)))
            v = v + dot(hh[:, 256:512], uw[cols, :], ((1,), (1,)))
            ig[k, :, :, :, :, cols] = v.reshape(4, 4, 2, 8, 512)
        return [push(ig.at[k, :, fs, 1 - c], core_in.at[k, :, fs], sibling)
                for fs in (pl.ds(2, 1), pl.ds(0, 2), pl.ds(3, 1))]

    def send_near(k, arrived):
        def terms(*fs):
            for n in range(4):
                for f in fs:
                    v = ig[k, n, f, c] + core_in[k, n, f]
                    v = jnp.concatenate([v[:, 0:512], v[:, 512:1024]], axis=0)
                    if n == 0:
                        near_own[k, f] = v
                    else:
                        near_out[k, n, f if n == 3 else PLACE[f]] = v.astype(BF16)

        def to(n, fs, dz):
            return push(near_out.at[k, n, fs], near_in.at[k, n, fs], along(dz))

        arrived[0].wait_recv()
        terms(2)
        early = [to(n, pl.ds(0, 1), NEAR[n]) for n in (1, 2)]
        for cp in arrived[1:]:
            cp.wait_recv()
        terms(0, 1, 3)
        late = [to(3, pl.ds(0, 2), 2), to(3, pl.ds(2, 2), -2)]
        return early, late + [to(n, pl.ds(1, 3), NEAR[n]) for n in (1, 2)]

    def send_far(k, early, late):
        out = []
        for cp in early:
            cp.wait_recv()
        for f in FAR_ORDER + (0,):
            if f == FAR_ORDER[1]:
                for cp in late:
                    cp.wait_recv()
            v = near_own[k, f]
            for n in (1, 2):
                v = v + near_in[k, n, PLACE[f]].astype(F32)
            if f < 2:
                v = v + near_in[k, 3, f].astype(F32)
            if f in (0, 3):
                v = v + near_in[k, 3, (f + 3) % 4].astype(F32)
            if k == 0 and f == 0:
                near_own[k, f] = v
            else:
                far_out[k, f] = v.astype(BF16)
                out.append(push(far_out.at[k, f], far_in.at[k, f],
                                along(4 * f, other_x=k == 1)))
        return out

    for cp in loads[2:]:
        cp.wait()
    for from_core, _, _, _ in shared:
        from_core.wait_recv()
    b0 = products(0)

    to_core = []
    for _, from_x, n, f in shared:
        from_x.wait_recv()
        other = x.at[c, 1, n, f]
        to_core.append(push(other, other, sibling))
    c0 = pointwise(0, b0)
    for cp in to_core:
        cp.wait_recv()
    b1 = products(1)

    c1 = pointwise(1, b1)
    i0 = input_products(0, c0)
    n0 = send_near(0, i0)
    i1 = input_products(1, c1)
    n1 = send_near(1, i1)
    spread_hidden = spread(0, hidden) + spread(1, hidden)
    f0 = send_far(0, *n0)
    f1 = send_far(1, *n1)

    for cp in spread_hidden:
        cp.wait_recv()
    factor = 1.0 / jnp.sqrt(F32(512))

    @pl.loop(0, 4)
    def _(i):
        cols = pl.ds(pl.multiple_of(i * 256, 256), 256)
        hh = h[...].reshape(512, 512)
        t = x[0, :, :, :, :, cols].reshape(512, 256)
        gg_ref[cols, :] = (dot(t, hh[:, 0:256], ((0,), (0,))) * factor).astype(BF16)
        ug_ref[cols, :] = (dot(t, hh[:, 256:512], ((0,), (0,))) * factor).astype(BF16)
        g = x[1, :, :, :, :, cols].reshape(512, 256)
        dg_ref[:, cols] = (dot(
            hidden[...].reshape(512, 256), g, ((0,), (0,))) * factor).astype(BF16)

    stores = [pltpu.make_async_copy(s, d, store_sem.at[i]) for i, (s, d) in enumerate((
        (gg_ref, gg_hbm), (ug_ref, ug_hbm), (dg_ref, dg_hbm), (ig_ref, ig_hbm)))]
    for cp in stores[:3]:
        cp.start()
    for cp in sent:
        cp.wait_send()
    for cp in f0 + f1:
        cp.wait_recv()
    v = near_own[0, 0] + far_in[1, 0].astype(F32)
    for f in (1, 2, 3):
        v = v + (far_in[0, f].astype(F32) + far_in[1, f].astype(F32))
    ig_ref[...] = jnp.concatenate([v[0:8], v[8:16]], axis=1).astype(BF16)

    stores[3].start()
    for cp in stores:
        cp.wait()


COPIES = 144


def place(*refs):
    given, wanted, held, load_sem, store_sem = refs[:4], refs[4:8], refs[8:12], refs[12], refs[13]
    loads, stores = [], []
    for s, v, d in zip(given, held, wanted):
        parts = 1 if s.shape[0] == 8 else 4
        rows = s.shape[0] // parts
        for i in range(parts):
            cut = pl.ds(i * rows, rows)
            k = len(loads)
            loads.append(pltpu.make_async_copy(s.at[cut], v.at[cut], load_sem.at[k]))
            stores.append(pltpu.make_async_copy(v.at[cut], d.at[cut], store_sem.at[k]))
    for cp in loads:
        cp.start()
    for load, store in zip(loads, stores):
        load.wait()
        store.start()
    for cp in stores:
        cp.wait()


def per_device(tokens, out_grad, gate_weight, up_weight, down_weight):
    hbm = pl.BlockSpec(memory_space=pl.ANY)
    shape = jax.ShapeDtypeStruct
    outs = (shape((8, 1024), BF16), shape((1024, 256), BF16),
            shape((1024, 256), BF16), shape((256, 1024), BF16))
    results = pl.pallas_call(
        kernel,
        out_shape=outs,
        in_specs=[hbm] * 5,
        out_specs=(hbm,) * 4,
        scratch_shapes=[
            pltpu.VMEM((8, 1024), BF16),
            pltpu.VMEM((8, 1024), BF16),
            pltpu.VMEM((1024, 256), BF16),
            pltpu.VMEM((1024, 256), BF16),
            pltpu.VMEM((256, 1024), BF16),
            pltpu.VMEM((8, 1024), F32),
            pltpu.VMEM((8, 1024), F32),
            pltpu.VMEM((2, 2, 4, 4, 16, 1024), BF16),
            pltpu.VMEM((2, 8, 32, 768), F32),
            pltpu.VMEM((2, 8, 32, 768), BF16),
            pltpu.VMEM((2, 7, 32, 768), BF16),
            pltpu.VMEM((2, 8, 32, 512), BF16),
            pltpu.VMEM((2, 8, 32, 256), BF16),
            pltpu.VMEM((2, 4, 4, 2, 8, 1024), F32),
            pltpu.VMEM((2, 4, 4, 8, 1024), F32),
            pltpu.VMEM((2, 4, 4, 16, 512), BF16),
            pltpu.VMEM((2, 4, 16, 512), F32),
            pltpu.VMEM((2, 4, 4, 16, 512), BF16),
            pltpu.VMEM((2, 4, 16, 512), BF16),
            pltpu.VMEM((2, 4, 16, 512), BF16),
            pltpu.VMEM((8, 1024), BF16),
            pltpu.VMEM((1024, 256), BF16),
            pltpu.VMEM((1024, 256), BF16),
            pltpu.VMEM((256, 1024), BF16),
            pltpu.SemaphoreType.DMA((5,)),
            pltpu.SemaphoreType.DMA((4,)),
            pltpu.SemaphoreType.DMA((COPIES,)),
            pltpu.SemaphoreType.DMA((COPIES,)),
        ],
        compiler_params=pltpu.CompilerParams(
            collective_id=0, has_side_effects=True, vmem_limit_bytes=60 << 20),
        cost_estimate=pl.CostEstimate(
            flops=2 * 8 * 512 * 1024 * 256, bytes_accessed=4 << 20, transcendentals=64 * 256),
    )(tokens, out_grad, gate_weight, up_weight, down_weight)
    return pl.pallas_call(
        place,
        out_shape=outs,
        in_specs=[hbm] * 4,
        out_specs=(hbm,) * 4,
        scratch_shapes=[pltpu.VMEM(o.shape, BF16) for o in outs]
        + [pltpu.SemaphoreType.DMA((13,))] * 2,
        compiler_params=pltpu.CompilerParams(vmem_limit_bytes=60 << 20),
    )(*results)


def solution(mesh):
    return jax.shard_map(
        per_device,
        mesh=mesh,
        in_specs=(P("gx", "gy"), P("gx", "gy"), P("gy", "gx"), P("gy", "gx"), P("gx", "gy")),
        out_specs=(P("gx", "gy"), P("gy", "gx"), P("gy", "gx"), P("gx", "gy")),
        check_vma=False,
    )
```
